32 devices in a mesh: groups: 2 (over x), seq: 8 (over z, y), role: 2 (over core).
Axes of the slice: x: 2, y: 2, z: 4, core: 2. Of those that a mesh axis runs over, the one named last changes fastest.
Arguments:
- pair_rep: bfloat16 [512, 256, 128], P(('groups', 'seq', 'role')), parts along dimension 0, may hold values from -6 to 6
- tri_gain: float32 [2, 128], replicated, may hold values from 0.1 to 1.9
- tri_proj: bfloat16 [2, 128, 512], replicated, may hold values from -0.5 to 0.5
- tri_gate: bfloat16 [2, 128, 128], replicated, may hold values from -0.5 to 0.5
- tri_mid_gain: float32 [2, 128], replicated, may hold values from 0.1 to 1.9
- tri_out: bfloat16 [2, 128, 128], replicated, may hold values from -0.5 to 0.5
- trans_gain: float32 [128], replicated, may hold values from 0.1 to 1.9
- trans_up: bfloat16 [128, 1024], replicated, may hold values from -0.5 to 0.5
- trans_down: bfloat16 [512, 128], replicated, may hold values from -0.25 to 0.25
Outputs:
- pair_out: bfloat16 [512, 256, 128], P(('groups', 'seq', 'role')), parts along dimension 0
The draws below stay inside these ranges and needn't reach their ends.
There are 2 independent parts, one for each index of `groups`. The reference program is written for one: setup_inputs(seed, part) draws one part's arguments, and reference() takes and returns one part's arrays. A program takes and returns all parts, laid end to end along the dimension named above; an argument that names none is the same for every part. Nothing has to cross between parts.
All inputs are finite; a program needn't handle non-finite values.
Results may differ from the reference program's by a relative error of at most 0.012.
Values may be sent and summed in bfloat16 or wider, within the bound.
No kernel may reach another device: no remote copies, remote signals or barrier semaphores. Data moves between devices by JAX's collectives and lax.ppermute only.
A program may use at most 64 MiB of HBM per device.

```python
import jax
import jax.numpy as jnp
from jax import lax

C = 128
CT = 128
H = 512
TOKENS = 256


def level_of(stream_key, extent, cuts, smallest, high):
    loudness, own = 1.0, jax.random.fold_in(stream_key, 6)
    for axis_at, shards_of in cuts:
        heights = jnp.exp(jax.random.uniform(jax.random.fold_in(own, axis_at), (shards_of,), jnp.float32, smallest / len(cuts), high / len(cuts)))
        loudness = loudness * jnp.repeat(heights, extent[axis_at] // shards_of).reshape([-1 if axis == axis_at else 1 for axis in range(len(extent))])
    return loudness


def noise(own_key, dims, scale, bound, pieces=(), kind=jnp.bfloat16):
    factor_of = level_of(own_key, dims, pieces, -0.22, 0.18) if pieces else 1.0
    entries = jax.random.normal(own_key, dims, jnp.float32) * scale * factor_of
    return jnp.minimum(jnp.maximum(entries, -bound), bound).astype(kind)


def setup_inputs(seed: int = 0, part: int = 0) -> dict:
    keys = jax.random.split(jax.random.key(seed), 10)
    own_keys = jax.random.split(jax.random.fold_in(keys[9], part), 10)
    pair_rep = noise(own_keys[0], (TOKENS, TOKENS, C), 1.0, 6.0, ((0, 16),))
    tri_gain = jnp.clip(1.0 + 0.18 * jax.random.normal(keys[1], (2, C), jnp.float32), 0.1, 1.9)
    tri_proj = noise(keys[2], (2, C, 4 * CT), C ** -0.5, 0.5)
    tri_gate = noise(keys[3], (2, C, C), C ** -0.5, 0.5)
    tri_mid_gain = jnp.clip(1.0 + 0.18 * jax.random.normal(keys[4], (2, CT), jnp.float32), 0.1, 1.9)
    tri_out = noise(keys[5], (2, CT, C), CT ** -0.5, 0.5)
    trans_gain = jnp.clip(1.0 + 0.18 * jax.random.normal(keys[6], (C,), jnp.float32), 0.1, 1.9)
    trans_up = noise(keys[7], (C, 2 * H), C ** -0.5, 0.5)
    trans_down = noise(keys[8], (H, C), H ** -0.5, 0.25)
    return dict(pair_rep=pair_rep, tri_gain=tri_gain, tri_proj=tri_proj, tri_gate=tri_gate, tri_mid_gain=tri_mid_gain, tri_out=tri_out, trans_gain=trans_gain, trans_up=trans_up, trans_down=trans_down)


epsilon = 1e-05

def layer_norm(values, gain):
    average = lax.optimization_barrier(jnp.mean(values, axis=-1, keepdims=True))
    centred = values - average
    spread = lax.optimization_barrier(jnp.mean(centred * centred, axis=-1, keepdims=True))
    return centred * lax.rsqrt(spread + epsilon) * gain

def reference(pair_rep, tri_gain, tri_proj, tri_gate, tri_mid_gain, tri_out, trans_gain, trans_up, trans_down):
    tokens_all = pair_rep.shape[0]
    channels = pair_rep.shape[2]
    inner = tri_out.shape[1]
    hidden_width = trans_down.shape[0]
    block_rows = 16
    block_count = tokens_all // block_rows
    current = pair_rep
    for which in range(2):

        def project(block_in):
            normed = layer_norm(block_in.astype(jnp.float32), tri_gain[which]).astype(jnp.bfloat16)
            projected = jnp.dot(normed, tri_proj[which], preferred_element_type=jnp.float32)
            left_side = (projected[..., :inner] * jax.nn.sigmoid(projected[..., inner:2 * inner])).astype(jnp.bfloat16)
            right_side = (projected[..., 2 * inner:3 * inner] * jax.nn.sigmoid(projected[..., 3 * inner:])).astype(jnp.bfloat16)
            gating = jax.nn.sigmoid(jnp.dot(normed, tri_gate[which], preferred_element_type=jnp.float32))
            return (left_side, right_side, gating)
        left_side, right_side, gating = lax.map(project, current.reshape(block_count, block_rows, tokens_all, channels))
        left_side = left_side.reshape(tokens_all, tokens_all, inner).astype(jnp.float32)
        right_side = right_side.reshape(tokens_all, tokens_all, inner).astype(jnp.float32)
        gating = gating.reshape(tokens_all, tokens_all, channels)
        if which == 0:
            product = jnp.einsum('ikc,jkc->ijc', left_side, right_side)
        else:
            product = jnp.einsum('kic,kjc->ijc', left_side, right_side)
        product = product.astype(jnp.bfloat16)
        normed_mid = layer_norm(product.astype(jnp.float32), tri_mid_gain[which]).astype(jnp.bfloat16)
        update = jnp.dot(normed_mid, tri_out[which], preferred_element_type=jnp.float32)
        current = (current.astype(jnp.float32) + gating * update).astype(jnp.bfloat16)

    def transition(block_in):
        normed = layer_norm(block_in.astype(jnp.float32), trans_gain).astype(jnp.bfloat16)
        values = jnp.dot(normed, trans_up, preferred_element_type=jnp.float32)
        hidden = (jax.nn.silu(values[..., :hidden_width]) * values[..., hidden_width:]).astype(jnp.bfloat16)
        down = jnp.dot(hidden, trans_down, preferred_element_type=jnp.float32)
        return (block_in.astype(jnp.float32) + down).astype(jnp.bfloat16)
    result = lax.map(transition, current.reshape(block_count, block_rows, tokens_all, channels))
    return result.reshape(tokens_all, tokens_all, channels)
```

```python
import functools

import jax
import jax.numpy as jnp
from jax import lax
from jax.experimental import pallas as pl
from jax.experimental.pallas import tpu as pltpu
from jax.sharding import PartitionSpec as P


epsilon = 1e-05
LANES = 128
VMEM_BYTES = 60 * 1024 * 1024
AXES = ("groups", "seq", "role")


def sigmoid(values):
    return 0.5 * jnp.tanh(0.5 * values) + 0.5


def norm_lanes(values, gain):
    average = jnp.mean(values, axis=-1, keepdims=True)
    centred = values - average
    spread = jnp.mean(centred * centred, axis=-1, keepdims=True)
    return (centred * lax.rsqrt(spread + epsilon) * gain).astype(jnp.bfloat16)


def dot(a, b, contract):
    return lax.dot_general(
        a, b, ((contract[:1], contract[1:]), ((), ())), preferred_element_type=jnp.float32
    )


def project(normed, proj_ref, sent_ref, scratch_ref, rows):
    parts, block, lanes = sent_ref.shape
    inner = proj_ref.shape[1] // 4
    half = block // 2
    for side in range(2):
        base = 2 * side * inner
        value = dot(proj_ref[:, base : base + inner], normed, (0, 1))
        gate = dot(proj_ref[:, base + inner : base + 2 * inner], normed, (0, 1))
        value = value * sigmoid(gate)
        for row in range(rows):
            scratch_ref[pl.ds(row, inner, stride=rows), :] = value[:, row * lanes : (row + 1) * lanes]
        sent_ref[:, side * half : (side + 1) * half] = (
            scratch_ref[: inner * rows].reshape(parts, half, lanes).astype(jnp.bfloat16)
        )


def combine(pair, rows, gain, gate_ref, mid_gain, out_ref, got_ref, scratch_ref):
    lanes = got_ref.shape[2]
    inner = out_ref.shape[0]
    got = got_ref[...].astype(jnp.float32).reshape(inner, rows, lanes)
    average = jnp.mean(got, axis=0, keepdims=True)
    centred = got - average
    spread = jnp.mean(centred * centred, axis=0, keepdims=True)
    scratch_ref[: inner * rows] = (centred * lax.rsqrt(spread + epsilon)).reshape(
        inner * rows, lanes
    )
    gating = sigmoid(dot(norm_lanes(pair, gain), gate_ref[...], (1, 0)))
    mid_gain = jnp.broadcast_to(mid_gain, (lanes, inner)).T
    updates = []
    for row in range(rows):
        mid = (scratch_ref[pl.ds(row, inner, stride=rows), :] * mid_gain).astype(jnp.bfloat16)
        updates.append(dot(mid, out_ref[...], (0, 0)))
    update = jnp.concatenate(updates, axis=0)
    return (pair + gating * update).astype(jnp.bfloat16)


def flat(pair):
    rows, lanes, channels = pair.shape
    return pair.astype(jnp.float32).reshape(rows * lanes, channels)


def first_kernel(
    flag_ref, own_ref, other_ref, gain_ref, proj_ref, pair_ref, sent_ref, scratch_ref
):
    rows = own_ref.shape[0]
    pair = jnp.where(flag_ref[0] == 1, flat(own_ref[...]), flat(other_ref[...]))
    pair_ref[...] = pair.astype(jnp.bfloat16).reshape(pair_ref.shape)
    project(norm_lanes(pair, gain_ref[0:1]), proj_ref, sent_ref, scratch_ref, rows)


def middle_kernel(
    near_ref, far_ref, got_ref, gain_ref, gate_ref, mid_gain_ref, out_ref, proj_ref,
    pair_out_ref, sent_ref, scratch_ref,
):
    rows = 2 * near_ref.shape[0]
    pair = jnp.concatenate([flat(near_ref[...]), flat(far_ref[...])], axis=0)
    current = combine(
        pair, rows, gain_ref[0:1], gate_ref, mid_gain_ref[0:1], out_ref, got_ref, scratch_ref
    )
    pair_out_ref[...] = current.reshape(pair_out_ref.shape)
    normed = norm_lanes(current.astype(jnp.float32), gain_ref[1:2])
    project(normed, proj_ref, sent_ref, scratch_ref, rows)


def last_kernel(
    pair_ref, got_ref, gain_ref, gate_ref, mid_gain_ref, out_ref, trans_gain_ref, up_ref, down_ref,
    pair_out_ref, scratch_ref,
):
    rows = pair_ref.shape[0]
    current = combine(
        flat(pair_ref[...]), rows, gain_ref[1:2], gate_ref, mid_gain_ref[1:2], out_ref, got_ref,
        scratch_ref,
    ).astype(jnp.float32)
    normed = norm_lanes(current, trans_gain_ref[...])
    hidden_width = down_ref.shape[0]
    total = current
    block = min(hidden_width, 2 * LANES)
    for start in range(0, hidden_width, block):
        gate = dot(normed, up_ref[:, start : start + block], (1, 0))
        value = dot(normed, up_ref[:, hidden_width + start : hidden_width + start + block], (1, 0))
        hidden = (gate * sigmoid(gate) * value).astype(jnp.bfloat16)
        total = total + dot(hidden, down_ref[start : start + block], (1, 0))
    pair_out_ref[...] = total.astype(jnp.bfloat16).reshape(pair_out_ref.shape)


def outgoing_kernel(side_ref, near_ref, far_ref, sent_ref):
    parts, block, width = near_ref.shape
    per, rows = sent_ref.shape[1], sent_ref.shape[2] // 2
    count = parts * rows
    side = side_ref[0]
    slots = [
        ref[...].astype(jnp.float32).reshape(parts, 2, per, rows, width)
        for ref in (near_ref, far_ref)
    ]
    for item in range(per):
        left, right = [
            [slot[:, which, item].reshape(count, width).astype(jnp.bfloat16) for slot in slots]
            for which in range(2)
        ]
        left = jnp.concatenate(left, axis=0)
        for slot in range(2):
            place = jnp.where(side == 0, slot, 1 - slot)
            part = dot(left, right[slot], (1, 1)).reshape(2, parts, rows, count)
            sent_ref[:, item, :, pl.ds(pl.multiple_of(place * count, LANES), count)] = (
                jnp.concatenate([part[0], part[1]], axis=1).astype(jnp.bfloat16)
            )


def incoming_kernel(side_ref, got_ref, sent_ref):
    parts, _, per, rows, width = got_ref.shape
    half = width // 2
    place = pl.ds(pl.multiple_of(side_ref[0] * half, LANES), half)
    own = rows // 2
    for item in range(per):
        left = got_ref[:, 0, item, :, place].reshape(parts * rows, half)
        right = got_ref[:, 1, item].reshape(parts * rows, width)
        sent_ref[:, item * own : (item + 1) * own] = dot(left, right, (0, 0)).reshape(
            parts, own, width
        ).astype(jnp.bfloat16)


def whole(shape):
    return pl.BlockSpec(shape, lambda step: (0,) * len(shape))


def one_of(shape, which):
    return pl.BlockSpec((None,) + shape, lambda step: (which,) + (0,) * len(shape))


def params():
    return pltpu.CompilerParams(vmem_limit_bytes=VMEM_BYTES)


def after(value, earlier):
    return lax.optimization_barrier((value, earlier))[0]


def local(
    pair_rep, tri_gain, tri_proj, tri_gate, tri_mid_gain, tri_out, trans_gain, trans_up, trans_down
):
    rows, width, channels = pair_rep.shape
    inner = tri_out.shape[1]
    groups, seq, role = (lax.axis_size(axis) for axis in AXES)
    half_seq = seq // 2
    parts = seq * role
    per = inner // parts
    own = rows // 2
    steps = width // LANES

    def number(g, s, c):
        return (g * seq + s) * role + c

    every = [(g, s, c) for g in range(groups) for s in range(seq) for c in range(role)]

    def at_home(g, s):
        return s // half_seq == g % 2

    def across(s):
        return (s + half_seq) % seq

    def permute(value, pairs):
        return lax.ppermute(value, AXES, [(number(*a), number(*b)) for a, b in pairs])

    blocks = [
        [
            number(base + u, side * half_seq + s, c)
            for s in range(half_seq)
            for c in range(role)
            for u in (side, 1 - side)
        ]
        for base in range(0, groups, 2)
        for side in range(2)
    ]

    def exchange(value):
        return lax.all_to_all(
            value, AXES, split_axis=0, concat_axis=0, tiled=True, axis_index_groups=blocks
        )

    side = lax.axis_index("seq") // half_seq
    home = side == lax.axis_index("groups") % 2
    side_flag = side.astype(jnp.int32).reshape(1)
    other_side_flag = 1 - side_flag
    home_flag = home.astype(jnp.int32).reshape(1)

    low, high = pair_rep[:own], pair_rep[own:]
    hopped = permute(high, [((g, s, c), (g ^ 1, s, c)) for g, s, c in every])
    direct = permute(low, [((g, s, c), (g, across(s), c)) for g, s, c in every if not at_home(g, s)])
    relayed = permute(hopped, [((g, s, c), (g, across(s), c)) for g, s, c in every if at_home(g, s)])

    flag_spec = pl.BlockSpec(memory_space=pltpu.SMEM)
    slot_spec = pl.BlockSpec((own, LANES, channels), lambda step: (0, step, 0))
    pair_spec = pl.BlockSpec((rows, LANES, channels), lambda step: (0, step, 0))
    gain_spec, mid_gain_spec = whole(tri_gain.shape), whole(tri_mid_gain.shape)
    scratch = [pltpu.VMEM((inner * rows, LANES), jnp.float32)]

    def shape(*dims):
        return jax.ShapeDtypeStruct(dims, jnp.bfloat16)

    def first(own_rows, other_rows, flops):
        return pl.pallas_call(
            first_kernel,
            grid=(steps,),
            in_specs=[
                flag_spec, slot_spec, slot_spec, gain_spec, one_of(tri_proj.shape[1:], 0),
            ],
            out_specs=[
                slot_spec,
                pl.BlockSpec((parts, 2 * per * own, LANES), lambda step: (0, 0, step)),
            ],
            out_shape=[shape(own, width, channels), shape(parts, 2 * per * own, width)],
            scratch_shapes=scratch,
            compiler_params=params(),
            cost_estimate=pl.CostEstimate(flops=flops, bytes_accessed=4 * 1024 * 1024, transcendentals=0),
            name="project",
        )(home_flag, own_rows, other_rows, tri_gain, tri_proj)

    near, near_sent = first(pair_rep, hopped, 0)
    near_got = exchange(near_sent)
    far, far_sent = first(direct, relayed, 20000000000)
    far_got = exchange(far_sent)

    product = pl.pallas_call(
        outgoing_kernel,
        in_specs=[flag_spec, pl.BlockSpec(), pl.BlockSpec()],
        out_specs=pl.BlockSpec(),
        out_shape=shape(parts, per, rows, width),
        compiler_params=params(),
        name="outgoing",
    )(side_flag, near_got, far_got)
    back = exchange(product).reshape(parts, per * rows, width)

    current, sent = pl.pallas_call(
        middle_kernel,
        grid=(steps,),
        in_specs=[
            slot_spec, slot_spec,
            pl.BlockSpec((parts, per * rows, LANES), lambda step: (0, 0, step)),
            gain_spec, one_of((channels, channels), 0), mid_gain_spec,
            one_of((inner, channels), 0), one_of(tri_proj.shape[1:], 1),
        ],
        out_specs=[
            pair_spec, pl.BlockSpec((parts, 2 * per * rows, LANES), lambda step: (0, 0, step)),
        ],
        out_shape=[shape(rows, width, channels), shape(parts, 2 * per * rows, width)],
        scratch_shapes=scratch,
        compiler_params=params(),
        name="combine_project",
    )(near, far, back, tri_gain, tri_gate, tri_mid_gain, tri_out, tri_proj)
    got = exchange(sent).reshape(parts, 2, per, rows, width)

    def incoming(flag, got):
        return pl.pallas_call(
            incoming_kernel,
            in_specs=[flag_spec, pl.BlockSpec()],
            out_specs=pl.BlockSpec(),
            out_shape=shape(parts, per * own, width),
            compiler_params=params(),
            name="incoming",
        )(flag, got)

    def last(slot, back):
        return pl.pallas_call(
            last_kernel,
            grid=(steps,),
            in_specs=[
                pl.BlockSpec((own, LANES, channels), lambda step: (slot, step, 0)),
                pl.BlockSpec((parts, per * own, LANES), lambda step: (0, 0, step)),
                gain_spec, one_of((channels, channels), 1), mid_gain_spec,
                one_of((inner, channels), 1), whole((1, channels)),
                whole(trans_up.shape), whole(trans_down.shape),
            ],
            out_specs=slot_spec,
            out_shape=shape(own, width, channels),
            scratch_shapes=scratch,
            compiler_params=params(),
            name="combine_transition",
        )(
            current, back, tri_gain, tri_gate, tri_mid_gain, tri_out, trans_gain[None],
            trans_up, trans_down,
        )

    far_product = incoming(other_side_flag, got)
    near_product = incoming(side_flag, after(got, far_product))
    far_back = exchange(far_product)
    near_back = exchange(after(near_product, far_back))
    far_out = last(1, far_back)
    near_out = last(0, near_back)

    from_home = permute(
        far_out, [((g, s, c), (g, across(s), c)) for g, s, c in every if at_home(g, s)]
    )
    from_away = permute(
        far_out, [((g, s, c), (g ^ 1, across(s), c)) for g, s, c in every if not at_home(g, s)]
    )
    from_near = permute(
        near_out, [((g, s, c), (g ^ 1, s, c)) for g, s, c in every if not at_home(g, s)]
    )
    return jnp.concatenate(
        [jnp.where(home, near_out, from_home), jnp.where(home, from_near, from_away)], axis=0
    )


def solution(mesh):
    in_specs = (P(AXES, None, None), P(), P(), P(), P(), P(), P(), P(), P())
    out_specs = P(AXES, None, None)
    return jax.shard_map(local, mesh=mesh, in_specs=in_specs, out_specs=out_specs, check_vma=False)
```

```python
import functools

import jax
import jax.numpy as jnp
from jax import lax
from jax.experimental import pallas as pl
from jax.experimental.pallas import tpu as pltpu
from jax.sharding import PartitionSpec as P


epsilon = 1e-05
LANES = 128
VMEM_BYTES = 24 * 1024 * 1024
DIAGONAL = 0
FAR_FLOPS = 20_000_000_000
AXES = ("groups", "seq", "role")


def sigmoid(values):
    return 0.5 * jnp.tanh(0.5 * values) + 0.5


def norm_lanes(values, gain):
    average = jnp.mean(values, axis=-1, keepdims=True)
    centred = values - average
    spread = jnp.mean(centred * centred, axis=-1, keepdims=True)
    return (centred * lax.rsqrt(spread + epsilon) * gain).astype(jnp.bfloat16)


def dot(a, b, contract):
    return lax.dot_general(
        a, b, ((contract[:1], contract[1:]), ((), ())), preferred_element_type=jnp.float32
    )


def column_blocks(width):
    return [slice(start, start + LANES) for start in range(0, width, LANES)]


def project(normed, proj_ref, which, sent_ref, columns, scratch_ref, rows):
    parts, block, _ = sent_ref.shape
    lanes = LANES
    inner = proj_ref.shape[2] // 4
    half = block // 2
    for side in range(2):
        base = 2 * side * inner
        value = dot(proj_ref[which, :, base : base + inner], normed, (0, 1))
        gate = dot(proj_ref[which, :, base + inner : base + 2 * inner], normed, (0, 1))
        value = value * sigmoid(gate)
        for row in range(rows):
            scratch_ref[pl.ds(row, inner, stride=rows), :] = value[:, row * lanes : (row + 1) * lanes]
        sent_ref[:, side * half : (side + 1) * half, columns] = (
            scratch_ref[: inner * rows].reshape(parts, half, lanes).astype(jnp.bfloat16)
        )


def combine(pair, rows, which, gain_ref, gate_ref, mid_gain_ref, out_ref, got, scratch_ref):
    lanes = got.shape[2]
    inner = out_ref.shape[1]
    got = got.astype(jnp.float32).reshape(inner, rows, lanes)
    average = jnp.mean(got, axis=0, keepdims=True)
    centred = got - average
    spread = jnp.mean(centred * centred, axis=0, keepdims=True)
    scratch_ref[: inner * rows] = (centred * lax.rsqrt(spread + epsilon)).reshape(
        inner * rows, lanes
    )
    normed = norm_lanes(pair, gain_ref[which : which + 1])
    gating = sigmoid(dot(normed, gate_ref[which], (1, 0)))
    mid_gain = jnp.broadcast_to(mid_gain_ref[which : which + 1], (lanes, inner)).T
    updates = []
    for row in range(rows):
        mid = (scratch_ref[pl.ds(row, inner, stride=rows), :] * mid_gain).astype(jnp.bfloat16)
        updates.append(dot(mid, out_ref[which], (0, 0)))
    update = jnp.concatenate(updates, axis=0)
    return (pair + gating * update).astype(jnp.bfloat16)


def flat(pair):
    rows, lanes, channels = pair.shape
    return pair.astype(jnp.float32).reshape(rows * lanes, channels)


def first_kernel(flag_ref, own_ref, gain_ref, proj_ref, *refs):
    other_refs, (pair_ref, sent_ref, scratch_ref) = refs[:-3], refs[-3:]
    rows, width, _ = pair_ref.shape
    for columns in column_blocks(width):
        other = jnp.concatenate([flat(ref[:, columns]) for ref in other_refs], axis=0)
        pair = jnp.where(flag_ref[0] == 1, flat(own_ref[:rows, columns]), other)
        pair_ref[:, columns] = pair.astype(jnp.bfloat16).reshape(rows, LANES, -1)
        normed = norm_lanes(pair, gain_ref[0:1])
        project(normed, proj_ref, 0, sent_ref, columns, scratch_ref, rows)


def middle_kernel(
    near_ref, far_ref, got_ref, gain_ref, gate_ref, mid_gain_ref, out_ref, proj_ref,
    pair_out_ref, sent_ref, scratch_ref,
):
    rows, width, _ = pair_out_ref.shape
    for columns in column_blocks(width):
        pair = jnp.concatenate([flat(near_ref[:, columns]), flat(far_ref[:, columns])], axis=0)
        current = combine(
            pair, rows, 0, gain_ref, gate_ref, mid_gain_ref, out_ref, got_ref[:, :, columns],
            scratch_ref,
        )
        pair_out_ref[:, columns] = current.reshape(rows, LANES, -1)
        normed = norm_lanes(current.astype(jnp.float32), gain_ref[1:2])
        project(normed, proj_ref, 1, sent_ref, columns, scratch_ref, rows)


def last_kernel(
    slot, pair_ref, got_ref, gain_ref, gate_ref, mid_gain_ref, out_ref, trans_gain_ref, up_ref,
    down_ref, pair_out_ref, scratch_ref,
):
    rows, width, _ = pair_out_ref.shape
    hidden_width = down_ref.shape[0]
    block = min(hidden_width, 2 * LANES)
    size = got_ref.shape[1] // 2
    for columns in column_blocks(width):
        got = got_ref[:, slot * size : (slot + 1) * size, columns]
        current = combine(
            flat(pair_ref[slot * rows : (slot + 1) * rows, columns]), rows, 1,
            gain_ref, gate_ref, mid_gain_ref, out_ref, got, scratch_ref,
        ).astype(jnp.float32)
        normed = norm_lanes(current, trans_gain_ref[...])
        total = current
        for start in range(0, hidden_width, block):
            stop = start + block
            gate = dot(normed, up_ref[:, start:stop], (1, 0))
            value = dot(normed, up_ref[:, hidden_width + start : hidden_width + stop], (1, 0))
            hidden = (gate * sigmoid(gate) * value).astype(jnp.bfloat16)
            total = total + dot(hidden, down_ref[start:stop], (1, 0))
        pair_out_ref[:, columns] = total.astype(jnp.bfloat16).reshape(rows, LANES, -1)


def outgoing_kernel(side_ref, near_ref, far_ref, sent_ref):
    parts, block, width = near_ref.shape
    per, rows = sent_ref.shape[1], sent_ref.shape[2] // 2
    count = parts * rows
    side = side_ref[0]
    slots = [
        ref[...].astype(jnp.float32).reshape(parts, 2, per, rows, width)
        for ref in (near_ref, far_ref)
    ]
    for item in range(per):
        left, right = [
            [slot[:, which, item].reshape(count, width).astype(jnp.bfloat16) for slot in slots]
            for which in range(2)
        ]
        left = jnp.concatenate(left, axis=0)
        for slot in range(2):
            place = jnp.where(side == 0, slot, 1 - slot)
            part = dot(left, right[slot], (1, 1)).reshape(2, parts, rows, count)
            sent_ref[:, item, :, pl.ds(pl.multiple_of(place * count, LANES), count)] = (
                jnp.concatenate([part[0], part[1]], axis=1).astype(jnp.bfloat16)
            )


def incoming_kernel(side_ref, got_ref, sent_ref):
    parts, _, per, rows, width = got_ref.shape
    half = width // 2
    own = rows // 2
    for item in range(per):
        right = got_ref[:, 1, item].reshape(parts * rows, width)
        for slot in range(2):
            side = side_ref[0] if slot == 0 else 1 - side_ref[0]
            place = pl.ds(pl.multiple_of(side * half, LANES), half)
            left = got_ref[:, 0, item, :, place].reshape(parts * rows, half)
            start = (slot * per + item) * own
            sent_ref[:, start : start + own] = (
                dot(left, right, (0, 0)).reshape(parts, own, width).astype(jnp.bfloat16)
            )


def join_kernel(top_ref, bottom_ref, out_ref):
    rows = top_ref.shape[0]
    out_ref[:rows] = top_ref[...]
    out_ref[rows:] = bottom_ref[...]


def pick_kernel(flag_ref, top_ref, bottom_ref, far_ref, out_ref):
    rows = top_ref.shape[0]

    @pl.when(flag_ref[0] == 1)
    def _():
        out_ref[:rows] = top_ref[...]
        out_ref[rows:] = bottom_ref[...]

    @pl.when(flag_ref[0] == 0)
    def _():
        out_ref[...] = far_ref[...]


def call(kernel, name, out_shape, scratch, *operands, flops=0):
    vmem = pl.BlockSpec(memory_space=pltpu.VMEM)
    smem = pl.BlockSpec(memory_space=pltpu.SMEM)
    several = isinstance(out_shape, (list, tuple))
    return pl.pallas_call(
        kernel,
        in_specs=[smem if operand.dtype == jnp.int32 else vmem for operand in operands],
        out_specs=[vmem] * len(out_shape) if several else vmem,
        out_shape=out_shape,
        scratch_shapes=scratch,
        compiler_params=pltpu.CompilerParams(vmem_limit_bytes=VMEM_BYTES),
        cost_estimate=pl.CostEstimate(flops=flops, bytes_accessed=0, transcendentals=0),
        name=name,
    )(*operands)


def after(value, earlier):
    return lax.optimization_barrier((value, earlier))[0]


def local(
    pair_rep, tri_gain, tri_proj, tri_gate, tri_mid_gain, tri_out, trans_gain, trans_up, trans_down
):
    rows, width, channels = pair_rep.shape
    inner = tri_out.shape[1]
    groups, seq, role = (lax.axis_size(axis) for axis in AXES)
    half_seq = seq // 2
    parts = seq * role
    per = inner // parts
    own = rows // 2

    def number(g, s, c):
        return (g * seq + s) * role + c

    every = [(g, s, c) for g in range(groups) for s in range(seq) for c in range(role)]

    def at_home(g, s):
        return s // half_seq == g % 2

    def across(s):
        return (s + half_seq) % seq

    def permute(value, pairs):
        return lax.ppermute(value, AXES, [(number(*a), number(*b)) for a, b in pairs])

    blocks = [
        [
            number(base + u, side * half_seq + s, c)
            for s in range(half_seq)
            for c in range(role)
            for u in (side, 1 - side)
        ]
        for base in range(0, groups, 2)
        for side in range(2)
    ]

    def exchange(value):
        return lax.all_to_all(
            value, AXES, split_axis=0, concat_axis=0, tiled=True, axis_index_groups=blocks
        )

    side = lax.axis_index("seq") // half_seq
    home = side == lax.axis_index("groups") % 2
    side_flag = side.astype(jnp.int32).reshape(1)
    other_side_flag = 1 - side_flag
    home_flag = home.astype(jnp.int32).reshape(1)

    low, high = pair_rep[:own], pair_rep[own:]
    hopped = permute(high, [((g, s, c), (g ^ 1, s, c)) for g, s, c in every])
    direct = permute(low, [((g, s, c), (g, across(s), c)) for g, s, c in every if not at_home(g, s)])
    cut = own * DIAGONAL // 8
    diagonal = permute(
        high[:cut],
        [((g, s, c), (g ^ 1, across(s), c)) for g, s, c in every if not at_home(g, s)],
    )
    relayed = permute(hopped[cut:], [((g, s, c), (g, across(s), c)) for g, s, c in every if at_home(g, s)])

    scratch = [pltpu.VMEM((inner * rows, LANES), jnp.float32)]

    def shape(*dims):
        return jax.ShapeDtypeStruct(dims, jnp.bfloat16)

    def first(own_rows, other_rows, flops):
        return call(
            first_kernel, "project",
            [shape(own, width, channels), shape(parts, 2 * per * own, width)], scratch,
            home_flag, own_rows, tri_gain, tri_proj, *other_rows, flops=flops,
        )

    near, near_sent = first(low, [hopped], 0)
    near_got = exchange(near_sent)
    far, far_sent = first(direct, [relayed], FAR_FLOPS)
    far_got = exchange(far_sent)

    product = call(
        outgoing_kernel, "outgoing", shape(parts, per, rows, width), [],
        side_flag, near_got, far_got,
    )
    back = exchange(product).reshape(parts, per * rows, width)

    current, sent = call(
        middle_kernel, "combine_project",
        [shape(rows, width, channels), shape(parts, 2 * per * rows, width)], scratch,
        near, far, back, tri_gain, tri_gate, tri_mid_gain, tri_out, tri_proj,
    )
    got = exchange(sent).reshape(parts, 2, per, rows, width)

    product = call(
        incoming_kernel, "incoming", shape(parts, per * rows, width), [], side_flag, got
    )
    back = exchange(product)

    def last(slot, back, flops):
        return call(
            functools.partial(last_kernel, slot), "combine_transition",
            shape(own, width, channels), scratch,
            current, back, tri_gain, tri_gate, tri_mid_gain, tri_out, trans_gain[None],
            trans_up, trans_down, flops=flops,
        )

    far_out = last(1, back, 0)
    near_out = last(0, after(back, far_out), FAR_FLOPS)

    from_home = permute(
        far_out, [((g, s, c), (g, across(s), c)) for g, s, c in every if at_home(g, s)]
    )
    from_away = permute(
        far_out, [((g, s, c), (g ^ 1, across(s), c)) for g, s, c in every if not at_home(g, s)]
    )
    from_near = permute(
        near_out, [((g, s, c), (g ^ 1, s, c)) for g, s, c in every if not at_home(g, s)]
    )
    far = call(join_kernel, "join", shape(rows, width, channels), [], from_home, from_away)
    return call(pick_kernel, "pick", shape(rows, width, channels), [], home_flag, near_out, from_near, far, flops=0)


def solution(mesh):
    in_specs = (P(AXES, None, None), P(), P(), P(), P(), P(), P(), P(), P())
    out_specs = P(AXES, None, None)
    return jax.shard_map(local, mesh=mesh, in_specs=in_specs, out_specs=out_specs, check_vma=False)
```

```python
import functools

import jax
import jax.numpy as jnp
from jax import lax
from jax.experimental import pallas as pl
from jax.experimental.pallas import tpu as pltpu
from jax.sharding import PartitionSpec as P


epsilon = 1e-05
LANES = 128
VMEM_BYTES = 24 * 1024 * 1024
SHARES = (8, 1, 3, 4)
FAR_FLOPS = 20_000_000_000
AXES = ("groups", "seq", "role")


def norm_lanes(values, gain):
    channels = values.shape[-1]
    share = jnp.full((channels, channels), 1.0 / channels, jnp.bfloat16)
    centred = values.astype(jnp.float32) - dot(values, share, (1, 0))
    spread = jnp.mean(centred * centred, axis=-1, keepdims=True)
    return (centred * lax.rsqrt(spread + epsilon) * gain).astype(jnp.bfloat16)


def dot(a, b, contract):
    return lax.dot_general(
        a, b, ((contract[:1], contract[1:]), ((), ())), preferred_element_type=jnp.float32
    )


def column_blocks(width):
    return [slice(start, start + LANES) for start in range(0, width, LANES)]


def project(normed, proj_ref, which, sent_ref, columns, rows, first=0):
    parts = sent_ref.shape[0]
    lanes = LANES
    inner = proj_ref.shape[2] // 4
    half = inner // parts * rows
    for side in range(2):
        base = 2 * side * inner
        both = dot(proj_ref[which, :, base : base + 2 * inner], normed, (0, 1))
        value = (both[:inner] * jax.nn.sigmoid(both[inner:])).astype(jnp.bfloat16)
        value = jnp.stack([value[:, row * lanes : (row + 1) * lanes] for row in range(rows)])
        start = first + side * half
        sent_ref[:, start : start + half, columns] = jnp.swapaxes(value, 0, 1).reshape(
            parts, half, lanes
        )


def combine(pair, rows, which, gain_ref, gate_ref, mid_gain_ref, out_ref, got, scratch_ref):
    lanes = got.shape[2]
    inner = out_ref.shape[1]
    got = got.astype(jnp.float32).reshape(inner, rows, lanes)
    average = jnp.mean(got, axis=0, keepdims=True)
    centred = got - average
    spread = jnp.mean(centred * centred, axis=0, keepdims=True)
    scratch_ref[: inner * rows] = (centred * lax.rsqrt(spread + epsilon)).reshape(
        inner * rows, lanes
    )
    normed = norm_lanes(pair, gain_ref[which : which + 1])
    gating = jax.nn.sigmoid(dot(normed, gate_ref[which], (1, 0)))
    mid_gain = jnp.broadcast_to(mid_gain_ref[which : which + 1], (lanes, inner)).T
    updates = []
    for row in range(rows):
        mid = (scratch_ref[pl.ds(row, inner, stride=rows), :] * mid_gain).astype(jnp.bfloat16)
        updates.append(dot(mid, out_ref[which], (0, 0)))
    update = jnp.concatenate(updates, axis=0)
    return (pair.astype(jnp.float32) + gating * update).astype(jnp.bfloat16)


def flat(pair):
    rows, lanes, channels = pair.shape
    return pair.reshape(rows * lanes, channels)


def near_kernel(flag_ref, own_ref, gain_ref, proj_ref, *refs):
    other_refs, (pair_ref, sent_ref) = refs[:-2], refs[-2:]
    rows, width, _ = pair_ref.shape
    for columns in column_blocks(width):
        other = jnp.concatenate([flat(ref[:, columns]) for ref in other_refs], axis=0)
        pair = jnp.where(flag_ref[0] == 1, flat(own_ref[:rows, columns]), other)
        pair_ref[:, columns] = pair.reshape(rows, LANES, -1)
        project(norm_lanes(pair, gain_ref[0:1]), proj_ref, 0, sent_ref, columns, rows)


def far_kernel(flag_ref, near_ref, own_ref, gain_ref, proj_ref, *refs):
    other_refs, (pair_ref, sent_ref) = refs[:-2], refs[-2:]
    rows, width, _ = pair_ref.shape
    first = near_ref.shape[1]
    sent_ref[:, :first] = near_ref[...]
    for columns in column_blocks(width):
        other = jnp.concatenate([flat(ref[:, columns]) for ref in other_refs], axis=0)
        pair = jnp.where(flag_ref[0] == 1, flat(own_ref[:rows, columns]), other)
        pair_ref[:, columns] = pair.reshape(rows, LANES, -1)
        project(norm_lanes(pair, gain_ref[0:1]), proj_ref, 0, sent_ref, columns, rows, first)


def middle_kernel(
    near_ref, far_ref, got_ref, gain_ref, gate_ref, mid_gain_ref, out_ref, proj_ref,
    pair_out_ref, sent_ref, scratch_ref,
):
    rows, width, _ = pair_out_ref.shape
    for columns in column_blocks(width):
        pair = jnp.concatenate([flat(near_ref[:, columns]), flat(far_ref[:, columns])], axis=0)
        current = combine(
            pair, rows, 0, gain_ref, gate_ref, mid_gain_ref, out_ref, got_ref[:, :, columns],
            scratch_ref,
        )
        pair_out_ref[:, columns] = current.reshape(rows, LANES, -1)
        normed = norm_lanes(current, gain_ref[1:2])
        project(normed, proj_ref, 1, sent_ref, columns, rows)


def last_kernel(
    slot, pair_ref, got_ref, gain_ref, gate_ref, mid_gain_ref, out_ref, trans_gain_ref, up_ref,
    down_ref, pair_out_ref, scratch_ref,
):
    rows, width, _ = pair_out_ref.shape
    hidden_width = down_ref.shape[0]
    block = min(hidden_width, 2 * LANES)
    size = got_ref.shape[1] // 2
    for columns in column_blocks(width):
        got = got_ref[:, slot * size : (slot + 1) * size, columns]
        current = combine(
            flat(pair_ref[slot * rows : (slot + 1) * rows, columns]), rows, 1,
            gain_ref, gate_ref, mid_gain_ref, out_ref, got, scratch_ref,
        )
        normed = norm_lanes(current, trans_gain_ref[...])
        total = current.astype(jnp.float32)
        for start in range(0, hidden_width, block):
            stop = start + block
            gate = dot(normed, up_ref[:, start:stop], (1, 0))
            value = dot(normed, up_ref[:, hidden_width + start : hidden_width + stop], (1, 0))
            hidden = (gate * jax.nn.sigmoid(gate) * value).astype(jnp.bfloat16)
            total = total + dot(hidden, down_ref[start:stop], (1, 0))
        pair_out_ref[:, columns] = total.astype(jnp.bfloat16).reshape(rows, LANES, -1)


def outgoing_kernel(side_ref, got_ref, sent_ref):
    parts, block, width = got_ref.shape
    block = block // 2
    per, rows = sent_ref.shape[1], sent_ref.shape[2] // 2
    count = parts * rows
    side = side_ref[0]
    slots = [
        part.astype(jnp.float32).reshape(parts, 2, per, rows, width)
        for part in (got_ref[:, :block], got_ref[:, block:])
    ]
    for item in range(per):
        left, right = [
            [slot[:, which, item].reshape(count, width).astype(jnp.bfloat16) for slot in slots]
            for which in range(2)
        ]
        left = jnp.concatenate(left, axis=0)
        for slot in range(2):
            place = jnp.where(side == 0, slot, 1 - slot)
            part = dot(left, right[slot], (1, 1)).reshape(2, parts, rows, count)
            sent_ref[:, item, :, pl.ds(pl.multiple_of(place * count, LANES), count)] = (
                jnp.concatenate([part[0], part[1]], axis=1).astype(jnp.bfloat16)
            )


def incoming_kernel(side_ref, got_ref, sent_ref):
    parts, _, per, rows, width = got_ref.shape
    half = width // 2
    own = rows // 2
    for item in range(per):
        right = got_ref[:, 1, item].reshape(parts * rows, width)
        for slot in range(2):
            side = side_ref[0] if slot == 0 else 1 - side_ref[0]
            place = pl.ds(pl.multiple_of(side * half, LANES), half)
            left = got_ref[:, 0, item, :, place].reshape(parts * rows, half)
            start = (slot * per + item) * own
            sent_ref[:, start : start + own] = (
                dot(left, right, (0, 0)).reshape(parts, own, width).astype(jnp.bfloat16)
            )


def join_kernel(top_ref, bottom_ref, out_ref):
    rows = top_ref.shape[0]
    out_ref[rows:] = top_ref[...]
    out_ref[:rows] = bottom_ref[...]


def pick_kernel(flag_ref, top_ref, bottom_ref, far_ref, out_ref):
    rows = top_ref.shape[0]

    @pl.when(flag_ref[0] == 1)
    def _():
        out_ref[:rows] = top_ref[...]
        out_ref[rows:] = bottom_ref[...]

    @pl.when(flag_ref[0] == 0)
    def _():
        out_ref[...] = far_ref[...]


def split_kernel(pair_ref, *refs):
    out_refs, sems = refs[:-1], refs[-1]
    copies, start = [], 0
    for place, out_ref in enumerate(out_refs):
        height = out_ref.shape[0]
        source = pair_ref.at[pl.ds(start, height)]
        copies.append(pltpu.make_async_copy(source, out_ref, sems.at[place]))
        start += height
    for copy in copies:
        copy.start()
    for copy in copies:
        copy.wait()


def call(kernel, name, out_shape, scratch, *operands, flops=0):
    vmem = pl.BlockSpec(memory_space=pltpu.VMEM)
    smem = pl.BlockSpec(memory_space=pltpu.SMEM)
    several = isinstance(out_shape, (list, tuple))
    return pl.pallas_call(
        kernel,
        in_specs=[smem if operand.dtype == jnp.int32 else vmem for operand in operands],
        out_specs=[vmem] * len(out_shape) if several else vmem,
        out_shape=out_shape,
        scratch_shapes=scratch,
        compiler_params=pltpu.CompilerParams(vmem_limit_bytes=VMEM_BYTES),
        cost_estimate=pl.CostEstimate(flops=flops, bytes_accessed=0, transcendentals=0),
        name=name,
    )(*operands)


def after(value, earlier):
    return lax.optimization_barrier((value, earlier))[0]


def local(
    pair_rep, tri_gain, tri_proj, tri_gate, tri_mid_gain, tri_out, trans_gain, trans_up, trans_down
):
    rows, width, channels = pair_rep.shape
    inner = tri_out.shape[1]
    groups, seq, role = (lax.axis_size(axis) for axis in AXES)
    half_seq = seq // 2
    parts = seq * role
    per = inner // parts
    own = rows // 2

    def number(g, s, c):
        return (g * seq + s) * role + c

    every = [(g, s, c) for g in range(groups) for s in range(seq) for c in range(role)]

    def at_home(g, s):
        return s // half_seq == g % 2

    def across(s):
        return (s + half_seq) % seq

    def permute(value, pairs):
        return lax.ppermute(value, AXES, [(number(*a), number(*b)) for a, b in pairs])

    blocks = [
        [
            number(base + u, side * half_seq + s, c)
            for s in range(half_seq)
            for c in range(role)
            for u in (side, 1 - side)
        ]
        for base in range(0, groups, 2)
        for side in range(2)
    ]

    def exchange(value):
        return lax.all_to_all(
            value, AXES, split_axis=0, concat_axis=0, tiled=True, axis_index_groups=blocks
        )

    side = lax.axis_index("seq") // half_seq
    home = side == lax.axis_index("groups") % 2
    side_flag = side.astype(jnp.int32).reshape(1)
    other_side_flag = 1 - side_flag
    home_flag = home.astype(jnp.int32).reshape(1)

    def shape(*dims):
        return jax.ShapeDtypeStruct(dims, jnp.bfloat16)

    heights = [own * share // 8 for share in SHARES]
    away = [(g, s, c) for g, s, c in every if not at_home(g, s)]
    low, middle, *high = pl.pallas_call(
        split_kernel,
        in_specs=[pl.BlockSpec(memory_space=pltpu.HBM)],
        out_specs=[pl.BlockSpec(memory_space=pltpu.VMEM)] * len(heights),
        out_shape=[shape(height, width, channels) for height in heights],
        scratch_shapes=[pltpu.SemaphoreType.DMA((len(heights),))],
        compiler_params=pltpu.CompilerParams(vmem_limit_bytes=VMEM_BYTES),
        name="split",
    )(pltpu.with_memory_space_constraint(pair_rep, pltpu.HBM))
    hopped = [permute(part, [((g, s, c), (g ^ 1, s, c)) for g, s, c in every]) for part in high]
    direct = permute(low, [((g, s, c), (g, across(s), c)) for g, s, c in away])
    relayed = [
        permute(part, [((g, s, c), (g, across(s), c)) for g, s, c in every if at_home(g, s)])
        for part in hopped
    ]
    diagonal = permute(middle, [((g, s, c), (g ^ 1, across(s), c)) for g, s, c in away])
    stepped = permute(middle, [((g, s, c), (g ^ 1, s, c)) for g, s, c in every if at_home(g, s)])

    scratch = [pltpu.VMEM((inner * rows, LANES), jnp.float32)]

    near, near_sent = call(
        near_kernel, "project",
        [shape(own, width, channels), shape(parts, 2 * per * own, width)], [],
        home_flag, low, tri_gain, tri_proj, stepped, *hopped, flops=0,
    )
    far, sent = call(
        far_kernel, "project",
        [shape(own, width, channels), shape(parts, 2 * per * rows, width)], [],
        home_flag, near_sent, direct, tri_gain, tri_proj, diagonal, *relayed,
    )
    got = exchange(sent)

    product = call(
        outgoing_kernel, "outgoing", shape(parts, per, rows, width), [],
        side_flag, got,
    )
    back = exchange(product).reshape(parts, per * rows, width)

    current, sent = call(
        middle_kernel, "combine_project",
        [shape(rows, width, channels), shape(parts, 2 * per * rows, width)], scratch,
        near, far, back, tri_gain, tri_gate, tri_mid_gain, tri_out, tri_proj,
    )
    got = exchange(sent).reshape(parts, 2, per, rows, width)

    product = call(
        incoming_kernel, "incoming", shape(parts, per * rows, width), [], side_flag, got
    )
    back = exchange(product)

    def last(slot, back, flops):
        return call(
            functools.partial(last_kernel, slot), "combine_transition",
            shape(own, width, channels), scratch,
            current, back, tri_gain, tri_gate, tri_mid_gain, tri_out, trans_gain[None],
            trans_up, trans_down, flops=flops,
        )

    far_out = last(1, back, 0)
    near_out = last(0, after(back, far_out), FAR_FLOPS)

    from_home = permute(
        far_out, [((g, s, c), (g, across(s), c)) for g, s, c in every if at_home(g, s)]
    )
    from_away = permute(
        far_out, [((g, s, c), (g ^ 1, across(s), c)) for g, s, c in every if not at_home(g, s)]
    )
    from_near = permute(
        near_out, [((g, s, c), (g ^ 1, s, c)) for g, s, c in every if not at_home(g, s)]
    )
    far = call(join_kernel, "join", shape(rows, width, channels), [], from_away, from_home)
    return call(pick_kernel, "pick", shape(rows, width, channels), [], home_flag, near_out, from_near, far, flops=0)


def solution(mesh):
    in_specs = (P(AXES, None, None), P(), P(), P(), P(), P(), P(), P(), P())
    out_specs = P(AXES, None, None)
    return jax.shard_map(local, mesh=mesh, in_specs=in_specs, out_specs=out_specs, check_vma=False)
```

```python
import functools

import jax
import jax.numpy as jnp
from jax import lax
from jax.experimental import pallas as pl
from jax.experimental.pallas import tpu as pltpu
from jax.sharding import PartitionSpec as P


epsilon = 1e-05
LANES = 128
VMEM_BYTES = 24 * 1024 * 1024
SHARES = (8, 1, 3, 4)
FAR_FLOPS = 20_000_000_000
AXES = ("groups", "seq", "role")


def norm_lanes(values, gain):
    channels = values.shape[-1]
    share = jnp.full((channels, channels), 1.0 / channels, jnp.bfloat16)
    centred = values.astype(jnp.float32) - dot(values, share, (1, 0))
    spread = jnp.mean(centred * centred, axis=-1, keepdims=True)
    return (centred * lax.rsqrt(spread + epsilon) * gain).astype(jnp.bfloat16)


def dot(a, b, contract):
    return lax.dot_general(
        a, b, ((contract[:1], contract[1:]), ((), ())), preferred_element_type=jnp.float32
    )


def column_blocks(width):
    return [slice(start, start + LANES) for start in range(0, width, LANES)]


def project(normed, proj_ref, which, sent_ref, columns, rows, first=0):
    parts = sent_ref.shape[0]
    lanes = LANES
    inner = proj_ref.shape[2] // 4
    half = inner // parts * rows
    for side in range(2):
        base = 2 * side * inner
        both = dot(proj_ref[which, :, base : base + 2 * inner], normed, (0, 1))
        value = (both[:inner] * jax.nn.sigmoid(both[inner:])).astype(jnp.bfloat16)
        value = jnp.stack([value[:, row * lanes : (row + 1) * lanes] for row in range(rows)])
        start = first + side * half
        sent_ref[:, start : start + half, columns] = jnp.swapaxes(value, 0, 1).reshape(
            parts, half, lanes
        )


def combine(pair, rows, which, gain_ref, gate_ref, mid_gain_ref, out_ref, got, scratch_ref):
    lanes = got.shape[2]
    inner = out_ref.shape[1]
    got = got.astype(jnp.float32).reshape(inner, rows, lanes)
    average = jnp.mean(got, axis=0, keepdims=True)
    centred = got - average
    spread = jnp.mean(centred * centred, axis=0, keepdims=True)
    scratch_ref[: inner * rows] = (centred * lax.rsqrt(spread + epsilon)).reshape(
        inner * rows, lanes
    )
    normed = norm_lanes(pair, gain_ref[which : which + 1])
    gating = jax.nn.sigmoid(dot(normed, gate_ref[which], (1, 0)))
    mid_gain = jnp.broadcast_to(mid_gain_ref[which : which + 1], (lanes, inner)).T
    updates = []
    for row in range(rows):
        mid = (scratch_ref[pl.ds(row, inner, stride=rows), :] * mid_gain).astype(jnp.bfloat16)
        updates.append(dot(mid, out_ref[which], (0, 0)))
    update = jnp.concatenate(updates, axis=0)
    return (pair.astype(jnp.float32) + gating * update).astype(jnp.bfloat16)


def flat(pair):
    rows, lanes, channels = pair.shape
    return pair.reshape(rows * lanes, channels)


def near_kernel(flag_ref, own_ref, gain_ref, proj_ref, *refs):
    other_refs, (pair_ref, sent_ref) = refs[:-2], refs[-2:]
    rows, width, _ = pair_ref.shape
    for columns in column_blocks(width):
        other = jnp.concatenate([flat(ref[:, columns]) for ref in other_refs], axis=0)
        pair = jnp.where(flag_ref[0] == 1, flat(own_ref[:rows, columns]), other)
        pair_ref[:, columns] = pair.reshape(rows, LANES, -1)
        project(norm_lanes(pair, gain_ref[0:1]), proj_ref, 0, sent_ref, columns, rows)


def middle_kernel(
    near_ref, far_ref, got_ref, gain_ref, gate_ref, mid_gain_ref, out_ref, proj_ref,
    pair_out_ref, sent_ref, scratch_ref,
):
    rows, width, _ = pair_out_ref.shape
    for columns in column_blocks(width):
        pair = jnp.concatenate([flat(near_ref[:, columns]), flat(far_ref[:, columns])], axis=0)
        current = combine(
            pair, rows, 0, gain_ref, gate_ref, mid_gain_ref, out_ref, got_ref[:, :, columns],
            scratch_ref,
        )
        pair_out_ref[:, columns] = current.reshape(rows, LANES, -1)
        normed = norm_lanes(current, gain_ref[1:2])
        project(normed, proj_ref, 1, sent_ref, columns, rows)


def last_kernel(
    slot, pair_ref, got_ref, gain_ref, gate_ref, mid_gain_ref, out_ref, trans_gain_ref, up_ref,
    down_ref, pair_out_ref, scratch_ref,
):
    rows, width, _ = pair_out_ref.shape
    hidden_width = down_ref.shape[0]
    block = min(hidden_width, 2 * LANES)
    size = got_ref.shape[1] // 2
    for columns in column_blocks(width):
        got = got_ref[:, slot * size : (slot + 1) * size, columns]
        current = combine(
            flat(pair_ref[slot * rows : (slot + 1) * rows, columns]), rows, 1,
            gain_ref, gate_ref, mid_gain_ref, out_ref, got, scratch_ref,
        )
        normed = norm_lanes(current, trans_gain_ref[...])
        total = current.astype(jnp.float32)
        for start in range(0, hidden_width, block):
            stop = start + block
            gate = dot(normed, up_ref[:, start:stop], (1, 0))
            value = dot(normed, up_ref[:, hidden_width + start : hidden_width + stop], (1, 0))
            hidden = (gate * jax.nn.sigmoid(gate) * value).astype(jnp.bfloat16)
            total = total + dot(hidden, down_ref[start:stop], (1, 0))
        pair_out_ref[:, columns] = total.astype(jnp.bfloat16).reshape(rows, LANES, -1)


def outgoing_kernel(side_ref, near_ref, far_ref, sent_ref):
    parts, block, width = near_ref.shape
    per, rows = sent_ref.shape[1], sent_ref.shape[2] // 2
    count = parts * rows
    side = side_ref[0]
    slots = [
        ref[...].astype(jnp.float32).reshape(parts, 2, per, rows, width)
        for ref in (near_ref, far_ref)
    ]
    for item in range(per):
        left, right = [
            [slot[:, which, item].reshape(count, width).astype(jnp.bfloat16) for slot in slots]
            for which in range(2)
        ]
        left = jnp.concatenate(left, axis=0)
        for slot in range(2):
            place = jnp.where(side == 0, slot, 1 - slot)
            part = dot(left, right[slot], (1, 1)).reshape(2, parts, rows, count)
            sent_ref[:, item, :, pl.ds(pl.multiple_of(place * count, LANES), count)] = (
                jnp.concatenate([part[0], part[1]], axis=1).astype(jnp.bfloat16)
            )


def incoming_kernel(side_ref, got_ref, sent_ref):
    parts, _, per, rows, width = got_ref.shape
    half = width // 2
    own = rows // 2
    for item in range(per):
        right = got_ref[:, 1, item].reshape(parts * rows, width)
        for slot in range(2):
            side = side_ref[0] if slot == 0 else 1 - side_ref[0]
            place = pl.ds(pl.multiple_of(side * half, LANES), half)
            left = got_ref[:, 0, item, :, place].reshape(parts * rows, half)
            start = (slot * per + item) * own
            sent_ref[:, start : start + own] = (
                dot(left, right, (0, 0)).reshape(parts, own, width).astype(jnp.bfloat16)
            )


def join_kernel(top_ref, bottom_ref, out_ref):
    rows = top_ref.shape[0]
    out_ref[rows:] = top_ref[...]
    out_ref[:rows] = bottom_ref[...]


def pick_kernel(flag_ref, top_ref, bottom_ref, far_ref, out_ref):
    rows = top_ref.shape[0]

    @pl.when(flag_ref[0] == 1)
    def _():
        out_ref[:rows] = top_ref[...]
        out_ref[rows:] = bottom_ref[...]

    @pl.when(flag_ref[0] == 0)
    def _():
        out_ref[...] = far_ref[...]


def split_kernel(pair_ref, proj_ref, gain_ref, *refs):
    (*out_refs, proj_out_ref, gain_out_ref), sems = refs[:-1], refs[-1]
    moves, start = [(proj_ref, proj_out_ref), (gain_ref, gain_out_ref)], 0
    for out_ref in out_refs:
        height = out_ref.shape[0]
        moves.append((pair_ref.at[pl.ds(start, height)], out_ref))
        start += height
    copies = [
        pltpu.make_async_copy(*move, sems.at[place]) for place, move in enumerate(moves)
    ]
    for copy in copies:
        copy.start()
    for copy in copies:
        copy.wait()


def call(kernel, name, out_shape, scratch, *operands, flops=0):
    vmem = pl.BlockSpec(memory_space=pltpu.VMEM)
    smem = pl.BlockSpec(memory_space=pltpu.SMEM)
    several = isinstance(out_shape, (list, tuple))
    return pl.pallas_call(
        kernel,
        in_specs=[smem if operand.dtype == jnp.int32 else vmem for operand in operands],
        out_specs=[vmem] * len(out_shape) if several else vmem,
        out_shape=out_shape,
        scratch_shapes=scratch,
        compiler_params=pltpu.CompilerParams(vmem_limit_bytes=VMEM_BYTES),
        cost_estimate=pl.CostEstimate(flops=flops, bytes_accessed=0, transcendentals=0),
        name=name,
    )(*operands)


def after(value, earlier):
    return lax.optimization_barrier((value, earlier))[0]


def local(
    pair_rep, tri_gain, tri_proj, tri_gate, tri_mid_gain, tri_out, trans_gain, trans_up, trans_down
):
    rows, width, channels = pair_rep.shape
    inner = tri_out.shape[1]
    groups, seq, role = (lax.axis_size(axis) for axis in AXES)
    half_seq = seq // 2
    parts = seq * role
    per = inner // parts
    own = rows // 2

    def number(g, s, c):
        return (g * seq + s) * role + c

    every = [(g, s, c) for g in range(groups) for s in range(seq) for c in range(role)]

    def at_home(g, s):
        return s // half_seq == g % 2

    def across(s):
        return (s + half_seq) % seq

    def permute(value, pairs):
        return lax.ppermute(value, AXES, [(number(*a), number(*b)) for a, b in pairs])

    blocks = [
        [
            number(base + u, side * half_seq + s, c)
            for s in range(half_seq)
            for c in range(role)
            for u in (side, 1 - side)
        ]
        for base in range(0, groups, 2)
        for side in range(2)
    ]

    def exchange(value):
        return lax.all_to_all(
            value, AXES, split_axis=0, concat_axis=0, tiled=True, axis_index_groups=blocks
        )

    side = lax.axis_index("seq") // half_seq
    home = side == lax.axis_index("groups") % 2
    side_flag = side.astype(jnp.int32).reshape(1)
    other_side_flag = 1 - side_flag
    home_flag = home.astype(jnp.int32).reshape(1)

    def shape(*dims):
        return jax.ShapeDtypeStruct(dims, jnp.bfloat16)

    heights = [own * share // 8 for share in SHARES]
    away = [(g, s, c) for g, s, c in every if not at_home(g, s)]
    low, middle, *high, first_proj, first_gain = pl.pallas_call(
        split_kernel,
        in_specs=[pl.BlockSpec(memory_space=pltpu.HBM)] * 3,
        out_specs=[pl.BlockSpec(memory_space=pltpu.VMEM)] * (len(heights) + 2),
        out_shape=[shape(height, width, channels) for height in heights]
        + [jax.ShapeDtypeStruct(value.shape, value.dtype) for value in (tri_proj, tri_gain)],
        scratch_shapes=[pltpu.SemaphoreType.DMA((len(heights) + 2,))],
        compiler_params=pltpu.CompilerParams(vmem_limit_bytes=VMEM_BYTES),
        name="split",
    )(*(
        pltpu.with_memory_space_constraint(value, pltpu.HBM)
        for value in (pair_rep, tri_proj, tri_gain)
    ))
    hopped = [permute(part, [((g, s, c), (g ^ 1, s, c)) for g, s, c in every]) for part in high]
    direct = permute(low, [((g, s, c), (g, across(s), c)) for g, s, c in away])
    relayed = [
        permute(part, [((g, s, c), (g, across(s), c)) for g, s, c in every if at_home(g, s)])
        for part in hopped
    ]
    diagonal = permute(middle, [((g, s, c), (g ^ 1, across(s), c)) for g, s, c in away])
    stepped = permute(middle, [((g, s, c), (g ^ 1, s, c)) for g, s, c in every if at_home(g, s)])

    scratch = [pltpu.VMEM((inner * rows, LANES), jnp.float32)]

    near, near_sent = call(
        near_kernel, "project",
        [shape(own, width, channels), shape(parts, 2 * per * own, width)], [],
        home_flag, low, first_gain, first_proj, stepped, *hopped, flops=0,
    )
    near_got = exchange(near_sent)
    far, far_sent = call(
        near_kernel, "project",
        [shape(own, width, channels), shape(parts, 2 * per * own, width)], [],
        home_flag, direct, first_gain, first_proj, diagonal, *relayed, flops=5 * FAR_FLOPS,
    )
    far_got = exchange(far_sent)

    product = call(
        outgoing_kernel, "outgoing", shape(parts, per, rows, width), [],
        side_flag, near_got, far_got,
    )
    back = exchange(product).reshape(parts, per * rows, width)

    current, sent = call(
        middle_kernel, "combine_project",
        [shape(rows, width, channels), shape(parts, 2 * per * rows, width)], scratch,
        near, far, back, tri_gain, tri_gate, tri_mid_gain, tri_out, tri_proj,
    )
    got = exchange(sent).reshape(parts, 2, per, rows, width)

    product = call(
        incoming_kernel, "incoming", shape(parts, per * rows, width), [], side_flag, got
    )
    back = exchange(product)

    def last(slot, back, flops):
        return call(
            functools.partial(last_kernel, slot), "combine_transition",
            shape(own, width, channels), scratch,
            current, back, tri_gain, tri_gate, tri_mid_gain, tri_out, trans_gain[None],
            trans_up, trans_down, flops=flops,
        )

    far_out = last(1, back, 0)
    near_out = last(0, after(back, far_out), FAR_FLOPS)

    from_home = permute(
        far_out, [((g, s, c), (g, across(s), c)) for g, s, c in every if at_home(g, s)]
    )
    from_away = permute(
        far_out, [((g, s, c), (g ^ 1, across(s), c)) for g, s, c in every if not at_home(g, s)]
    )
    from_near = permute(
        near_out, [((g, s, c), (g ^ 1, s, c)) for g, s, c in every if not at_home(g, s)]
    )
    far = call(join_kernel, "join", shape(rows, width, channels), [], from_away, from_home)
    return call(pick_kernel, "pick", shape(rows, width, channels), [], home_flag, near_out, from_near, far, flops=0)


def solution(mesh):
    in_specs = (P(AXES, None, None), P(), P(), P(), P(), P(), P(), P(), P())
    out_specs = P(AXES, None, None)
    return jax.shard_map(local, mesh=mesh, in_specs=in_specs, out_specs=out_specs, check_vma=False)
```

```python
import functools

import jax
import jax.numpy as jnp
from jax import lax
from jax.experimental import pallas as pl
from jax.experimental.pallas import tpu as pltpu
from jax.sharding import PartitionSpec as P


epsilon = 1e-05
LANES = 128
VMEM_BYTES = 24 * 1024 * 1024
SHARES = (8, 1, 4, 3)
FAR_FLOPS = 20_000_000_000
AXES = ("groups", "seq", "role")


def norm_lanes(values, gain):
    channels = values.shape[-1]
    share = jnp.full((channels, channels), 1.0 / channels, jnp.bfloat16)
    centred = values.astype(jnp.float32) - dot(values, share, (1, 0))
    spread = jnp.mean(centred * centred, axis=-1, keepdims=True)
    return (centred * lax.rsqrt(spread + epsilon) * gain).astype(jnp.bfloat16)


def dot(a, b, contract):
    return lax.dot_general(
        a, b, ((contract[:1], contract[1:]), ((), ())), preferred_element_type=jnp.float32
    )


def column_blocks(width):
    return [slice(start, start + LANES) for start in range(0, width, LANES)]


def project(normed, proj_ref, which, sent_ref, columns, rows, first=0):
    parts = sent_ref.shape[0]
    lanes = LANES
    inner = proj_ref.shape[2] // 4
    half = inner // parts * rows
    for side in range(2):
        base = 2 * side * inner
        both = dot(proj_ref[which, :, base : base + 2 * inner], normed, (0, 1))
        value = (both[:inner] * jax.nn.sigmoid(both[inner:])).astype(jnp.bfloat16)
        value = jnp.stack([value[:, row * lanes : (row + 1) * lanes] for row in range(rows)])
        start = first + side * half
        sent_ref[:, start : start + half, columns] = jnp.swapaxes(value, 0, 1).reshape(
            parts, half, lanes
        )


def combine(pair, rows, which, gain_ref, gate_ref, mid_gain_ref, out_ref, got, scratch_ref):
    lanes = got.shape[2]
    inner = out_ref.shape[1]
    got = got.astype(jnp.float32).reshape(inner, rows, lanes)
    average = jnp.mean(got, axis=0, keepdims=True)
    centred = got - average
    spread = jnp.mean(centred * centred, axis=0, keepdims=True)
    scratch_ref[: inner * rows] = (centred * lax.rsqrt(spread + epsilon)).reshape(
        inner * rows, lanes
    )
    normed = norm_lanes(pair, gain_ref[which : which + 1])
    gating = jax.nn.sigmoid(dot(normed, gate_ref[which], (1, 0)))
    mid_gain = jnp.broadcast_to(mid_gain_ref[which : which + 1], (lanes, inner)).T
    updates = []
    for row in range(rows):
        mid = (scratch_ref[pl.ds(row, inner, stride=rows), :] * mid_gain).astype(jnp.bfloat16)
        updates.append(dot(mid, out_ref[which], (0, 0)))
    update = jnp.concatenate(updates, axis=0)
    return (pair.astype(jnp.float32) + gating * update).astype(jnp.bfloat16)


def flat(pair):
    rows, lanes, channels = pair.shape
    return pair.reshape(rows * lanes, channels)


def near_kernel(flag_ref, own_ref, gain_ref, proj_ref, *refs):
    other_refs, (pair_ref, sent_ref) = refs[:-2], refs[-2:]
    rows, width, _ = pair_ref.shape
    for columns in column_blocks(width):
        other = jnp.concatenate([flat(ref[:, columns]) for ref in other_refs], axis=0)
        pair = jnp.where(flag_ref[0] == 1, flat(own_ref[:rows, columns]), other)
        pair_ref[:, columns] = pair.reshape(rows, LANES, -1)
        project(norm_lanes(pair, gain_ref[0:1]), proj_ref, 0, sent_ref, columns, rows)


def middle_kernel(
    near_ref, far_ref, got_ref, gain_ref, gate_ref, mid_gain_ref, out_ref, proj_ref,
    pair_out_ref, sent_ref, scratch_ref,
):
    rows, width, _ = pair_out_ref.shape
    for columns in column_blocks(width):
        pair = jnp.concatenate([flat(near_ref[:, columns]), flat(far_ref[:, columns])], axis=0)
        current = combine(
            pair, rows, 0, gain_ref, gate_ref, mid_gain_ref, out_ref, got_ref[:, :, columns],
            scratch_ref,
        )
        pair_out_ref[:, columns] = current.reshape(rows, LANES, -1)
        normed = norm_lanes(current, gain_ref[1:2])
        project(normed, proj_ref, 1, sent_ref, columns, rows)


def last_kernel(
    slot, pair_ref, got_ref, gain_ref, gate_ref, mid_gain_ref, out_ref, trans_gain_ref, up_ref,
    down_ref, pair_out_ref, scratch_ref,
):
    rows, width, _ = pair_out_ref.shape
    hidden_width = down_ref.shape[0]
    block = min(hidden_width, 2 * LANES)
    size = got_ref.shape[1] // 2
    for columns in column_blocks(width):
        got = got_ref[:, slot * size : (slot + 1) * size, columns]
        current = combine(
            flat(pair_ref[slot * rows : (slot + 1) * rows, columns]), rows, 1,
            gain_ref, gate_ref, mid_gain_ref, out_ref, got, scratch_ref,
        )
        normed = norm_lanes(current, trans_gain_ref[...])
        total = current.astype(jnp.float32)
        for start in range(0, hidden_width, block):
            stop = start + block
            gate = dot(normed, up_ref[:, start:stop], (1, 0))
            value = dot(normed, up_ref[:, hidden_width + start : hidden_width + stop], (1, 0))
            hidden = (gate * jax.nn.sigmoid(gate) * value).astype(jnp.bfloat16)
            total = total + dot(hidden, down_ref[start:stop], (1, 0))
        pair_out_ref[:, columns] = total.astype(jnp.bfloat16).reshape(rows, LANES, -1)


def outgoing_kernel(side_ref, near_ref, far_ref, sent_ref):
    parts, block, width = near_ref.shape
    per, rows = sent_ref.shape[1], sent_ref.shape[2] // 2
    count = parts * rows
    side = side_ref[0]
    slots = [
        ref[...].astype(jnp.float32).reshape(parts, 2, per, rows, width)
        for ref in (near_ref, far_ref)
    ]
    for item in range(per):
        left, right = [
            [slot[:, which, item].reshape(count, width).astype(jnp.bfloat16) for slot in slots]
            for which in range(2)
        ]
        left = jnp.concatenate(left, axis=0)
        for slot in range(2):
            place = jnp.where(side == 0, slot, 1 - slot)
            part = dot(left, right[slot], (1, 1)).reshape(2, parts, rows, count)
            sent_ref[:, item, :, pl.ds(pl.multiple_of(place * count, LANES), count)] = (
                jnp.concatenate([part[0], part[1]], axis=1).astype(jnp.bfloat16)
            )


def incoming_kernel(side_ref, got_ref, sent_ref):
    parts, _, per, rows, width = got_ref.shape
    half = width // 2
    own = rows // 2
    for item in range(0, per, 2):
        pair = range(item, min(item + 2, per))
        right = [got_ref[:, 1, each].reshape(parts * rows, width) for each in pair]
        for slot in range(2):
            side = side_ref[0] if slot == 0 else 1 - side_ref[0]
            place = pl.ds(pl.multiple_of(side * half, LANES), half)
            left = [got_ref[:, 0, each, :, place].reshape(parts * rows, half) for each in pair]
            start = (slot * per + item) * own
            sent_ref[:, start : start + len(pair) * own] = jnp.concatenate(
                [
                    dot(one, other, (0, 0)).reshape(parts, own, width)
                    for one, other in zip(left, right)
                ],
                axis=1,
            ).astype(jnp.bfloat16)


def join_kernel(top_ref, bottom_ref, out_ref):
    rows = top_ref.shape[0]
    out_ref[rows:] = top_ref[...]
    out_ref[:rows] = bottom_ref[...]


def pick_kernel(flag_ref, top_ref, bottom_ref, far_ref, out_ref):
    rows = top_ref.shape[0]

    @pl.when(flag_ref[0] == 1)
    def _():
        out_ref[:rows] = top_ref[...]
        out_ref[rows:] = bottom_ref[...]

    @pl.when(flag_ref[0] == 0)
    def _():
        out_ref[...] = far_ref[...]


def split_kernel(pair_ref, proj_ref, gain_ref, *refs):
    (*out_refs, proj_out_ref, gain_out_ref), sems = refs[:-1], refs[-1]
    moves, start = [(proj_ref, proj_out_ref), (gain_ref, gain_out_ref)], 0
    for out_ref in out_refs:
        height = out_ref.shape[0]
        moves.append((pair_ref.at[pl.ds(start, height)], out_ref))
        start += height
    copies = [
        pltpu.make_async_copy(*move, sems.at[place]) for place, move in enumerate(moves)
    ]
    for copy in copies:
        copy.start()
    for copy in copies:
        copy.wait()


def call(kernel, name, out_shape, scratch, *operands, flops=0):
    vmem = pl.BlockSpec(memory_space=pltpu.VMEM)
    smem = pl.BlockSpec(memory_space=pltpu.SMEM)
    several = isinstance(out_shape, (list, tuple))
    return pl.pallas_call(
        kernel,
        in_specs=[smem if operand.dtype == jnp.int32 else vmem for operand in operands],
        out_specs=[vmem] * len(out_shape) if several else vmem,
        out_shape=out_shape,
        scratch_shapes=scratch,
        compiler_params=pltpu.CompilerParams(vmem_limit_bytes=VMEM_BYTES),
        cost_estimate=pl.CostEstimate(flops=flops, bytes_accessed=0, transcendentals=0),
        name=name,
    )(*operands)


def after(value, earlier):
    return lax.optimization_barrier((value, earlier))[0]


def local(
    pair_rep, tri_gain, tri_proj, tri_gate, tri_mid_gain, tri_out, trans_gain, trans_up, trans_down
):
    rows, width, channels = pair_rep.shape
    inner = tri_out.shape[1]
    groups, seq, role = (lax.axis_size(axis) for axis in AXES)
    half_seq = seq // 2
    parts = seq * role
    per = inner // parts
    own = rows // 2

    def number(g, s, c):
        return (g * seq + s) * role + c

    every = [(g, s, c) for g in range(groups) for s in range(seq) for c in range(role)]

    def at_home(g, s):
        return s // half_seq == g % 2

    def across(s):
        return (s + half_seq) % seq

    def permute(value, pairs):
        return lax.ppermute(value, AXES, [(number(*a), number(*b)) for a, b in pairs])

    blocks = [
        [
            number(base + u, side * half_seq + s, c)
            for s in range(half_seq)
            for c in range(role)
            for u in (side, 1 - side)
        ]
        for base in range(0, groups, 2)
        for side in range(2)
    ]

    def exchange(value):
        return lax.all_to_all(
            value, AXES, split_axis=0, concat_axis=0, tiled=True, axis_index_groups=blocks
        )

    side = lax.axis_index("seq") // half_seq
    home = side == lax.axis_index("groups") % 2
    side_flag = side.astype(jnp.int32).reshape(1)
    home_flag = home.astype(jnp.int32).reshape(1)

    def shape(*dims):
        return jax.ShapeDtypeStruct(dims, jnp.bfloat16)

    heights = [own * share // 8 for share in SHARES]
    away = [(g, s, c) for g, s, c in every if not at_home(g, s)]
    low, middle, *high, first_proj, first_gain = pl.pallas_call(
        split_kernel,
        in_specs=[pl.BlockSpec(memory_space=pltpu.HBM)] * 3,
        out_specs=[pl.BlockSpec(memory_space=pltpu.VMEM)] * (len(heights) + 2),
        out_shape=[shape(height, width, channels) for height in heights]
        + [jax.ShapeDtypeStruct(value.shape, value.dtype) for value in (tri_proj, tri_gain)],
        scratch_shapes=[pltpu.SemaphoreType.DMA((len(heights) + 2,))],
        compiler_params=pltpu.CompilerParams(vmem_limit_bytes=VMEM_BYTES),
        name="split",
    )(*(
        pltpu.with_memory_space_constraint(value, pltpu.HBM)
        for value in (pair_rep, tri_proj, tri_gain)
    ))
    hopped = [permute(part, [((g, s, c), (g ^ 1, s, c)) for g, s, c in every]) for part in high]
    direct = permute(low, [((g, s, c), (g, across(s), c)) for g, s, c in away])
    relayed = [
        permute(part, [((g, s, c), (g, across(s), c)) for g, s, c in every if at_home(g, s)])
        for part in hopped
    ]
    diagonal = permute(middle, [((g, s, c), (g ^ 1, across(s), c)) for g, s, c in away])
    stepped = permute(middle, [((g, s, c), (g ^ 1, s, c)) for g, s, c in every if at_home(g, s)])

    scratch = [pltpu.VMEM((inner * rows, LANES), jnp.float32)]

    near, near_sent = call(
        near_kernel, "project",
        [shape(own, width, channels), shape(parts, 2 * per * own, width)], [],
        home_flag, low, first_gain, first_proj, stepped, *hopped, flops=0,
    )
    near_got = exchange(near_sent)
    far, far_sent = call(
        near_kernel, "project",
        [shape(own, width, channels), shape(parts, 2 * per * own, width)], [],
        home_flag, direct, first_gain, first_proj, diagonal, *relayed, flops=5 * FAR_FLOPS,
    )
    far_got = exchange(far_sent)

    product = call(
        outgoing_kernel, "outgoing", shape(parts, per, rows, width), [],
        side_flag, near_got, far_got,
    )
    back = exchange(product).reshape(parts, per * rows, width)

    current, sent = call(
        middle_kernel, "combine_project",
        [shape(rows, width, channels), shape(parts, 2 * per * rows, width)], scratch,
        near, far, back, tri_gain, tri_gate, tri_mid_gain, tri_out, tri_proj,
    )
    got = exchange(sent).reshape(parts, 2, per, rows, width)

    product = call(
        incoming_kernel, "incoming", shape(parts, per * rows, width), [], side_flag, got
    )
    back = exchange(product)

    def last(slot, back, flops):
        return call(
            functools.partial(last_kernel, slot), "combine_transition",
            shape(own, width, channels), scratch,
            current, back, tri_gain, tri_gate, tri_mid_gain, tri_out, trans_gain[None],
            trans_up, trans_down, flops=flops,
        )

    far_out = last(1, back, 0)
    near_out = last(0, after(back, far_out), FAR_FLOPS)

    from_home = permute(
        far_out, [((g, s, c), (g, across(s), c)) for g, s, c in every if at_home(g, s)]
    )
    from_away = permute(
        far_out, [((g, s, c), (g ^ 1, across(s), c)) for g, s, c in every if not at_home(g, s)]
    )
    from_near = permute(
        near_out, [((g, s, c), (g ^ 1, s, c)) for g, s, c in every if not at_home(g, s)]
    )
    far = call(join_kernel, "join", shape(rows, width, channels), [], from_away, from_home)
    return call(
        pick_kernel, "pick", shape(rows, width, channels), [], home_flag, near_out, from_near, far
    )


def solution(mesh):
    in_specs = (P(AXES, None, None), P(), P(), P(), P(), P(), P(), P(), P())
    out_specs = P(AXES, None, None)
    return jax.shard_map(local, mesh=mesh, in_specs=in_specs, out_specs=out_specs, check_vma=False)
```

```python
import functools

import jax
import jax.numpy as jnp
from jax import lax
from jax.experimental import pallas as pl
from jax.experimental.pallas import tpu as pltpu
from jax.sharding import PartitionSpec as P


epsilon = 1e-05
LANES = 128
VMEM_BYTES = 24 * 1024 * 1024
SHARES = (8, 1, 4, 3)
FAR_FLOPS = 20_000_000_000
AXES = ("groups", "seq", "role")


def norm_lanes(values, gain):
    channels = values.shape[-1]
    share = jnp.full((channels, channels), 1.0 / channels, jnp.bfloat16)
    centred = values.astype(jnp.float32) - dot(values, share, (1, 0))
    spread = jnp.mean(centred * centred, axis=-1, keepdims=True)
    return (centred * lax.rsqrt(spread + epsilon) * gain).astype(jnp.bfloat16)


def dot(a, b, contract):
    return lax.dot_general(
        a, b, ((contract[:1], contract[1:]), ((), ())), preferred_element_type=jnp.float32
    )


def column_blocks(width):
    return [slice(start, start + LANES) for start in range(0, width, LANES)]


def project(normed, proj_ref, which, sent_ref, columns, rows, first=0):
    parts = sent_ref.shape[0]
    lanes = LANES
    inner = proj_ref.shape[2] // 4
    half = inner // parts * rows
    for side in range(2):
        base = 2 * side * inner
        both = dot(proj_ref[which, :, base : base + 2 * inner], normed, (0, 1))
        value = (both[:inner] * jax.nn.sigmoid(both[inner:])).astype(jnp.bfloat16)
        value = jnp.stack([value[:, row * lanes : (row + 1) * lanes] for row in range(rows)])
        start = first + side * half
        sent_ref[:, start : start + half, columns] = jnp.swapaxes(value, 0, 1).reshape(
            parts, half, lanes
        )


def combine(pair, rows, which, gain_ref, gate_ref, mid_gain_ref, out_ref, got, scratch_ref):
    lanes = got.shape[2]
    inner = out_ref.shape[1]
    got = got.astype(jnp.float32).reshape(inner, rows, lanes)
    average = jnp.mean(got, axis=0, keepdims=True)
    centred = got - average
    spread = jnp.mean(centred * centred, axis=0, keepdims=True)
    centred = centred * lax.rsqrt(spread + epsilon)
    normed = norm_lanes(pair, gain_ref[which : which + 1])
    gating = jax.nn.sigmoid(dot(normed, gate_ref[which], (1, 0)))
    mid_gain = jnp.broadcast_to(mid_gain_ref[which : which + 1], (lanes, inner)).T
    if rows % 16 == 0:
        mids = jnp.swapaxes((centred * mid_gain.reshape(inner, 1, lanes)).astype(jnp.bfloat16), 0, 1)
        mids = [mids[row] for row in range(rows)]
    else:
        scratch_ref[: inner * rows] = centred.reshape(inner * rows, lanes)
        mids = [
            (scratch_ref[pl.ds(row, inner, stride=rows), :] * mid_gain).astype(jnp.bfloat16)
            for row in range(rows)
        ]
    updates = [dot(mid, out_ref[which], (0, 0)) for mid in mids]
    update = jnp.concatenate(updates, axis=0)
    return (pair.astype(jnp.float32) + gating * update).astype(jnp.bfloat16)


def flat(pair):
    rows, lanes, channels = pair.shape
    return pair.reshape(rows * lanes, channels)


def near_kernel(flag_ref, own_ref, gain_ref, proj_ref, *refs):
    other_refs, (pair_ref, sent_ref) = refs[:-2], refs[-2:]
    rows, width, _ = pair_ref.shape
    for columns in column_blocks(width):
        other = jnp.concatenate([flat(ref[:, columns]) for ref in other_refs], axis=0)
        pair = jnp.where(flag_ref[0] == 1, flat(own_ref[:rows, columns]), other)
        pair_ref[:, columns] = pair.reshape(rows, LANES, -1)
        project(norm_lanes(pair, gain_ref[0:1]), proj_ref, 0, sent_ref, columns, rows)


def middle_kernel(
    near_ref, far_ref, got_ref, gain_ref, gate_ref, mid_gain_ref, out_ref, proj_ref,
    pair_out_ref, sent_ref, scratch_ref,
):
    rows, width, _ = pair_out_ref.shape
    for columns in column_blocks(width):
        pair = jnp.concatenate([flat(near_ref[:, columns]), flat(far_ref[:, columns])], axis=0)
        current = combine(
            pair, rows, 0, gain_ref, gate_ref, mid_gain_ref, out_ref, got_ref[:, :, columns],
            scratch_ref,
        )
        pair_out_ref[:, columns] = current.reshape(rows, LANES, -1)
        normed = norm_lanes(current, gain_ref[1:2])
        project(normed, proj_ref, 1, sent_ref, columns, rows)


def last_kernel(
    slot, pair_ref, got_ref, gain_ref, gate_ref, mid_gain_ref, out_ref, trans_gain_ref, up_ref,
    down_ref, pair_out_ref, scratch_ref,
):
    rows, width, _ = pair_out_ref.shape
    hidden_width = down_ref.shape[0]
    block = min(hidden_width, 2 * LANES)
    size = got_ref.shape[1] // 2
    for columns in column_blocks(width):
        got = got_ref[:, slot * size : (slot + 1) * size, columns]
        current = combine(
            flat(pair_ref[slot * rows : (slot + 1) * rows, columns]), rows, 1,
            gain_ref, gate_ref, mid_gain_ref, out_ref, got, scratch_ref,
        )
        normed = norm_lanes(current, trans_gain_ref[...])
        total = current.astype(jnp.float32)
        for start in range(0, hidden_width, block):
            stop = start + block
            gate = dot(normed, up_ref[:, start:stop], (1, 0))
            value = dot(normed, up_ref[:, hidden_width + start : hidden_width + stop], (1, 0))
            hidden = (gate * jax.nn.sigmoid(gate) * value).astype(jnp.bfloat16)
            total = total + dot(hidden, down_ref[start:stop], (1, 0))
        pair_out_ref[:, columns] = total.astype(jnp.bfloat16).reshape(rows, LANES, -1)


def outgoing_kernel(side_ref, near_ref, far_ref, sent_ref):
    parts, block, width = near_ref.shape
    per, rows = sent_ref.shape[1], sent_ref.shape[2] // 2
    count = parts * rows
    side = side_ref[0]
    slots = [
        ref[...].astype(jnp.float32).reshape(parts, 2, per, rows, width)
        for ref in (near_ref, far_ref)
    ]
    for item in range(per):
        left, right = [
            [slot[:, which, item].reshape(count, width).astype(jnp.bfloat16) for slot in slots]
            for which in range(2)
        ]
        left = jnp.concatenate(left, axis=0)
        for slot in range(2):
            place = jnp.where(side == 0, slot, 1 - slot)
            part = dot(left, right[slot], (1, 1)).reshape(2, parts, rows, count)
            sent_ref[:, item, :, pl.ds(pl.multiple_of(place * count, LANES), count)] = (
                jnp.concatenate([part[0], part[1]], axis=1).astype(jnp.bfloat16)
            )


def incoming_kernel(side_ref, got_ref, sent_ref):
    parts, _, per, rows, width = got_ref.shape
    half = width // 2
    own = rows // 2
    for item in range(0, per, 2):
        pair = range(item, min(item + 2, per))
        right = [got_ref[:, 1, each].reshape(parts * rows, width) for each in pair]
        for slot in range(2):
            side = side_ref[0] if slot == 0 else 1 - side_ref[0]
            place = pl.ds(pl.multiple_of(side * half, LANES), half)
            left = [got_ref[:, 0, each, :, place].reshape(parts * rows, half) for each in pair]
            start = (slot * per + item) * own
            sent_ref[:, start : start + len(pair) * own] = jnp.concatenate(
                [
                    dot(one, other, (0, 0)).reshape(parts, own, width)
                    for one, other in zip(left, right)
                ],
                axis=1,
            ).astype(jnp.bfloat16)


def join_kernel(top_ref, bottom_ref, out_ref):
    rows = top_ref.shape[0]
    out_ref[rows:] = top_ref[...]
    out_ref[:rows] = bottom_ref[...]


def pick_kernel(flag_ref, top_ref, bottom_ref, far_ref, out_ref):
    rows = top_ref.shape[0]

    @pl.when(flag_ref[0] == 1)
    def _():
        out_ref[:rows] = top_ref[...]
        out_ref[rows:] = bottom_ref[...]

    @pl.when(flag_ref[0] == 0)
    def _():
        out_ref[...] = far_ref[...]


def split_kernel(pair_ref, proj_ref, gain_ref, *refs):
    (*out_refs, proj_out_ref, gain_out_ref), sems = refs[:-1], refs[-1]
    moves, start = [(proj_ref, proj_out_ref), (gain_ref, gain_out_ref)], 0
    for out_ref in out_refs:
        height = out_ref.shape[0]
        moves.append((pair_ref.at[pl.ds(start, height)], out_ref))
        start += height
    copies = [
        pltpu.make_async_copy(*move, sems.at[place]) for place, move in enumerate(moves)
    ]
    for copy in copies:
        copy.start()
    for copy in copies:
        copy.wait()


def call(kernel, name, out_shape, scratch, *operands, flops=0):
    vmem = pl.BlockSpec(memory_space=pltpu.VMEM)
    smem = pl.BlockSpec(memory_space=pltpu.SMEM)
    several = isinstance(out_shape, (list, tuple))
    return pl.pallas_call(
        kernel,
        in_specs=[smem if operand.dtype == jnp.int32 else vmem for operand in operands],
        out_specs=[vmem] * len(out_shape) if several else vmem,
        out_shape=out_shape,
        scratch_shapes=scratch,
        compiler_params=pltpu.CompilerParams(vmem_limit_bytes=VMEM_BYTES),
        cost_estimate=pl.CostEstimate(flops=flops, bytes_accessed=0, transcendentals=0),
        name=name,
    )(*operands)


def after(value, earlier):
    return lax.optimization_barrier((value, earlier))[0]


def local(
    pair_rep, tri_gain, tri_proj, tri_gate, tri_mid_gain, tri_out, trans_gain, trans_up, trans_down
):
    rows, width, channels = pair_rep.shape
    inner = tri_out.shape[1]
    groups, seq, role = (lax.axis_size(axis) for axis in AXES)
    half_seq = seq // 2
    parts = seq * role
    per = inner // parts
    own = rows // 2

    def number(g, s, c):
        return (g * seq + s) * role + c

    every = [(g, s, c) for g in range(groups) for s in range(seq) for c in range(role)]

    def at_home(g, s):
        return s // half_seq == g % 2

    def across(s):
        return (s + half_seq) % seq

    def permute(value, pairs):
        return lax.ppermute(value, AXES, [(number(*a), number(*b)) for a, b in pairs])

    blocks = [
        [
            number(base + u, side * half_seq + s, c)
            for s in range(half_seq)
            for c in range(role)
            for u in (side, 1 - side)
        ]
        for base in range(0, groups, 2)
        for side in range(2)
    ]

    def exchange(value):
        return lax.all_to_all(
            value, AXES, split_axis=0, concat_axis=0, tiled=True, axis_index_groups=blocks
        )

    side = lax.axis_index("seq") // half_seq
    home = side == lax.axis_index("groups") % 2
    side_flag = side.astype(jnp.int32).reshape(1)
    home_flag = home.astype(jnp.int32).reshape(1)

    def shape(*dims):
        return jax.ShapeDtypeStruct(dims, jnp.bfloat16)

    heights = [own * share // 8 for share in SHARES]
    away = [(g, s, c) for g, s, c in every if not at_home(g, s)]
    low, middle, *high, first_proj, first_gain = pl.pallas_call(
        split_kernel,
        in_specs=[pl.BlockSpec(memory_space=pltpu.HBM)] * 3,
        out_specs=[pl.BlockSpec(memory_space=pltpu.VMEM)] * (len(heights) + 2),
        out_shape=[shape(height, width, channels) for height in heights]
        + [jax.ShapeDtypeStruct(value.shape, value.dtype) for value in (tri_proj, tri_gain)],
        scratch_shapes=[pltpu.SemaphoreType.DMA((len(heights) + 2,))],
        compiler_params=pltpu.CompilerParams(vmem_limit_bytes=VMEM_BYTES),
        name="split",
    )(*(
        pltpu.with_memory_space_constraint(value, pltpu.HBM)
        for value in (pair_rep, tri_proj, tri_gain)
    ))
    hopped = [permute(part, [((g, s, c), (g ^ 1, s, c)) for g, s, c in every]) for part in high]
    direct = permute(low, [((g, s, c), (g, across(s), c)) for g, s, c in away])
    relayed = [
        permute(part, [((g, s, c), (g, across(s), c)) for g, s, c in every if at_home(g, s)])
        for part in hopped
    ]
    diagonal = permute(middle, [((g, s, c), (g ^ 1, across(s), c)) for g, s, c in away])
    stepped = permute(middle, [((g, s, c), (g ^ 1, s, c)) for g, s, c in every if at_home(g, s)])

    scratch = [pltpu.VMEM((inner * rows, LANES), jnp.float32)]

    near, near_sent = call(
        near_kernel, "project",
        [shape(own, width, channels), shape(parts, 2 * per * own, width)], [],
        home_flag, low, first_gain, first_proj, stepped, *hopped, flops=0,
    )
    near_got = exchange(near_sent)
    far, far_sent = call(
        near_kernel, "project",
        [shape(own, width, channels), shape(parts, 2 * per * own, width)], [],
        home_flag, direct, first_gain, first_proj, diagonal, *relayed, flops=5 * FAR_FLOPS,
    )
    far_got = exchange(far_sent)

    product = call(
        outgoing_kernel, "outgoing", shape(parts, per, rows, width), [],
        side_flag, near_got, far_got,
    )
    back = exchange(product).reshape(parts, per * rows, width)

    current, sent = call(
        middle_kernel, "combine_project",
        [shape(rows, width, channels), shape(parts, 2 * per * rows, width)], scratch,
        near, far, back, tri_gain, tri_gate, tri_mid_gain, tri_out, tri_proj,
    )
    got = exchange(sent).reshape(parts, 2, per, rows, width)

    product = call(
        incoming_kernel, "incoming", shape(parts, per * rows, width), [], side_flag, got
    )
    back = exchange(product)

    def last(slot, back, flops):
        return call(
            functools.partial(last_kernel, slot), "combine_transition",
            shape(own, width, channels), scratch,
            current, back, tri_gain, tri_gate, tri_mid_gain, tri_out, trans_gain[None],
            trans_up, trans_down, flops=flops,
        )

    far_out = last(1, back, 0)
    near_out = last(0, after(back, far_out), FAR_FLOPS)

    from_home = permute(
        far_out, [((g, s, c), (g, across(s), c)) for g, s, c in every if at_home(g, s)]
    )
    from_away = permute(
        far_out, [((g, s, c), (g ^ 1, across(s), c)) for g, s, c in every if not at_home(g, s)]
    )
    from_near = permute(
        near_out, [((g, s, c), (g ^ 1, s, c)) for g, s, c in every if not at_home(g, s)]
    )
    far = call(join_kernel, "join", shape(rows, width, channels), [], from_away, from_home)
    return call(
        pick_kernel, "pick", shape(rows, width, channels), [], home_flag, near_out, from_near, far
    )


def solution(mesh):
    in_specs = (P(AXES, None, None), P(), P(), P(), P(), P(), P(), P(), P())
    out_specs = P(AXES, None, None)
    return jax.shard_map(local, mesh=mesh, in_specs=in_specs, out_specs=out_specs, check_vma=False)
```

```python
import functools

import jax
import jax.numpy as jnp
from jax import lax
from jax.experimental import pallas as pl
from jax.experimental.pallas import tpu as pltpu
from jax.sharding import PartitionSpec as P


epsilon = 1e-05
LANES = 128
VMEM_BYTES = 24 * 1024 * 1024
SHARES = (8, 1, 4, 3)
FAR_FLOPS = 20_000_000_000
AXES = ("groups", "seq", "role")


def norm_lanes(values, gain):
    channels = values.shape[-1]
    share = jnp.full((channels, channels), 1.0 / channels, jnp.bfloat16)
    centred = values.astype(jnp.float32) - dot(values, share, (1, 0))
    spread = jnp.mean(centred * centred, axis=-1, keepdims=True)
    return (centred * lax.rsqrt(spread + epsilon) * gain).astype(jnp.bfloat16)


def dot(a, b, contract):
    return lax.dot_general(
        a, b, ((contract[:1], contract[1:]), ((), ())), preferred_element_type=jnp.float32
    )


def column_blocks(width):
    return [slice(start, start + LANES) for start in range(0, width, LANES)]


def project(normed, proj_ref, which, sent_ref, columns, rows, first=0):
    parts = sent_ref.shape[0]
    lanes = LANES
    inner = proj_ref.shape[2] // 4
    half = inner // parts * rows
    for side in range(2):
        base = 2 * side * inner
        both = dot(proj_ref[which, :, base : base + 2 * inner], normed, (0, 1))
        value = (both[:inner] * jax.nn.sigmoid(both[inner:])).astype(jnp.bfloat16)
        value = jnp.stack([value[:, row * lanes : (row + 1) * lanes] for row in range(rows)])
        start = first + side * half
        sent_ref[:, start : start + half, columns] = jnp.swapaxes(value, 0, 1).reshape(
            parts, half, lanes
        )


def combine(pair, normed, rows, which, gate_ref, mid_gain_ref, out_ref, got, scratch_ref):
    lanes = got.shape[2]
    inner = out_ref.shape[1]
    got = got.astype(jnp.float32).reshape(inner, rows, lanes)
    average = jnp.mean(got, axis=0, keepdims=True)
    centred = got - average
    spread = jnp.mean(centred * centred, axis=0, keepdims=True)
    centred = centred * lax.rsqrt(spread + epsilon)
    gating = jax.nn.sigmoid(dot(normed, gate_ref[which], (1, 0)))
    mid_gain = jnp.broadcast_to(mid_gain_ref[which : which + 1], (lanes, inner)).T
    if rows % 16 == 0:
        mids = jnp.swapaxes((centred * mid_gain.reshape(inner, 1, lanes)).astype(jnp.bfloat16), 0, 1)
        mids = [mids[row] for row in range(rows)]
    else:
        scratch_ref[: inner * rows] = centred.reshape(inner * rows, lanes)
        mids = [
            (scratch_ref[pl.ds(row, inner, stride=rows), :] * mid_gain).astype(jnp.bfloat16)
            for row in range(rows)
        ]
    updates = [dot(mid, out_ref[which], (0, 0)) for mid in mids]
    update = jnp.concatenate(updates, axis=0)
    return (pair.astype(jnp.float32) + gating * update).astype(jnp.bfloat16)


def flat(pair):
    rows, lanes, channels = pair.shape
    return pair.reshape(rows * lanes, channels)


def near_kernel(flag_ref, own_ref, gain_ref, proj_ref, *refs):
    other_refs, (pair_ref, normed_ref, sent_ref) = refs[:-3], refs[-3:]
    rows, width, _ = pair_ref.shape
    for columns in column_blocks(width):
        other = jnp.concatenate([flat(ref[:, columns]) for ref in other_refs], axis=0)
        pair = jnp.where(flag_ref[0] == 1, flat(own_ref[:rows, columns]), other)
        pair_ref[:, columns] = pair.reshape(rows, LANES, -1)
        normed = norm_lanes(pair, gain_ref[0:1])
        normed_ref[:, columns] = normed.reshape(rows, LANES, -1)
        project(normed, proj_ref, 0, sent_ref, columns, rows)


def middle_kernel(
    near_ref, far_ref, near_normed_ref, far_normed_ref, got_ref, gain_ref, gate_ref, mid_gain_ref, out_ref, proj_ref,
    pair_out_ref, normed_ref, sent_ref, scratch_ref,
):
    rows, width, _ = pair_out_ref.shape
    for columns in column_blocks(width):
        pair = jnp.concatenate([flat(near_ref[:, columns]), flat(far_ref[:, columns])], axis=0)
        normed = jnp.concatenate(
            [flat(near_normed_ref[:, columns]), flat(far_normed_ref[:, columns])], axis=0
        )
        current = combine(
            pair, normed, rows, 0, gate_ref, mid_gain_ref, out_ref, got_ref[:, :, columns],
            scratch_ref,
        )
        pair_out_ref[:, columns] = current.reshape(rows, LANES, -1)
        normed = norm_lanes(current, gain_ref[1:2])
        normed_ref[:, columns] = normed.reshape(rows, LANES, -1)
        project(normed, proj_ref, 1, sent_ref, columns, rows)


def last_kernel(
    slot, pair_ref, normed_ref, got_ref, gate_ref, mid_gain_ref, out_ref, trans_gain_ref, up_ref,
    down_ref, pair_out_ref, scratch_ref,
):
    rows, width, _ = pair_out_ref.shape
    hidden_width = down_ref.shape[0]
    block = min(hidden_width, 2 * LANES)
    size = got_ref.shape[1] // 2
    for columns in column_blocks(width):
        got = got_ref[:, slot * size : (slot + 1) * size, columns]
        current = combine(
            flat(pair_ref[slot * rows : (slot + 1) * rows, columns]),
            flat(normed_ref[slot * rows : (slot + 1) * rows, columns]), rows, 1, gate_ref, mid_gain_ref, out_ref, got, scratch_ref,
        )
        normed = norm_lanes(current, trans_gain_ref[...])
        total = current.astype(jnp.float32)
        for start in range(0, hidden_width, block):
            stop = start + block
            gate = dot(normed, up_ref[:, start:stop], (1, 0))
            value = dot(normed, up_ref[:, hidden_width + start : hidden_width + stop], (1, 0))
            hidden = (gate * jax.nn.sigmoid(gate) * value).astype(jnp.bfloat16)
            total = total + dot(hidden, down_ref[start:stop], (1, 0))
        pair_out_ref[:, columns] = total.astype(jnp.bfloat16).reshape(rows, LANES, -1)


def outgoing_kernel(side_ref, near_ref, far_ref, sent_ref):
    parts, block, width = near_ref.shape
    per, rows = sent_ref.shape[1], sent_ref.shape[2] // 2
    count = parts * rows
    side = side_ref[0]
    slots = [
        ref[...].astype(jnp.float32).reshape(parts, 2, per, rows, width)
        for ref in (near_ref, far_ref)
    ]
    for item in range(per):
        left, right = [
            [slot[:, which, item].reshape(count, width).astype(jnp.bfloat16) for slot in slots]
            for which in range(2)
        ]
        left = jnp.concatenate(left, axis=0)
        for slot in range(2):
            place = jnp.where(side == 0, slot, 1 - slot)
            part = dot(left, right[slot], (1, 1)).reshape(2, parts, rows, count)
            sent_ref[:, item, :, pl.ds(pl.multiple_of(place * count, LANES), count)] = (
                jnp.concatenate([part[0], part[1]], axis=1).astype(jnp.bfloat16)
            )


def incoming_kernel(side_ref, got_ref, sent_ref):
    parts, _, per, rows, width = got_ref.shape
    half = width // 2
    own = rows // 2
    for item in range(0, per, 2):
        pair = range(item, min(item + 2, per))
        right = [got_ref[:, 1, each].reshape(parts * rows, width) for each in pair]
        for slot in range(2):
            side = side_ref[0] if slot == 0 else 1 - side_ref[0]
            place = pl.ds(pl.multiple_of(side * half, LANES), half)
            left = [got_ref[:, 0, each, :, place].reshape(parts * rows, half) for each in pair]
            start = (slot * per + item) * own
            sent_ref[:, start : start + len(pair) * own] = jnp.concatenate(
                [
                    dot(one, other, (0, 0)).reshape(parts, own, width)
                    for one, other in zip(left, right)
                ],
                axis=1,
            ).astype(jnp.bfloat16)


def join_kernel(top_ref, bottom_ref, out_ref):
    rows = top_ref.shape[0]
    out_ref[rows:] = top_ref[...]
    out_ref[:rows] = bottom_ref[...]


def pick_kernel(flag_ref, top_ref, bottom_ref, far_ref, out_ref):
    rows = top_ref.shape[0]

    @pl.when(flag_ref[0] == 1)
    def _():
        out_ref[:rows] = top_ref[...]
        out_ref[rows:] = bottom_ref[...]

    @pl.when(flag_ref[0] == 0)
    def _():
        out_ref[...] = far_ref[...]


def split_kernel(pair_ref, proj_ref, gain_ref, *refs):
    (*out_refs, proj_out_ref, gain_out_ref), sems = refs[:-1], refs[-1]
    moves, start = [(proj_ref, proj_out_ref), (gain_ref, gain_out_ref)], 0
    for out_ref in out_refs:
        height = out_ref.shape[0]
        moves.append((pair_ref.at[pl.ds(start, height)], out_ref))
        start += height
    copies = [
        pltpu.make_async_copy(*move, sems.at[place]) for place, move in enumerate(moves)
    ]
    for copy in copies:
        copy.start()
    for copy in copies:
        copy.wait()


def call(kernel, name, out_shape, scratch, *operands, flops=0):
    vmem = pl.BlockSpec(memory_space=pltpu.VMEM)
    smem = pl.BlockSpec(memory_space=pltpu.SMEM)
    several = isinstance(out_shape, (list, tuple))
    return pl.pallas_call(
        kernel,
        in_specs=[smem if operand.dtype == jnp.int32 else vmem for operand in operands],
        out_specs=[vmem] * len(out_shape) if several else vmem,
        out_shape=out_shape,
        scratch_shapes=scratch,
        compiler_params=pltpu.CompilerParams(vmem_limit_bytes=VMEM_BYTES),
        cost_estimate=pl.CostEstimate(flops=flops, bytes_accessed=0, transcendentals=0),
        name=name,
    )(*operands)


def after(value, earlier):
    return lax.optimization_barrier((value, earlier))[0]


def local(
    pair_rep, tri_gain, tri_proj, tri_gate, tri_mid_gain, tri_out, trans_gain, trans_up, trans_down
):
    rows, width, channels = pair_rep.shape
    inner = tri_out.shape[1]
    groups, seq, role = (lax.axis_size(axis) for axis in AXES)
    half_seq = seq // 2
    parts = seq * role
    per = inner // parts
    own = rows // 2

    def number(g, s, c):
        return (g * seq + s) * role + c

    every = [(g, s, c) for g in range(groups) for s in range(seq) for c in range(role)]

    def at_home(g, s):
        return s // half_seq == g % 2

    def across(s):
        return (s + half_seq) % seq

    def permute(value, pairs):
        return lax.ppermute(value, AXES, [(number(*a), number(*b)) for a, b in pairs])

    blocks = [
        [
            number(base + u, side * half_seq + s, c)
            for s in range(half_seq)
            for c in range(role)
            for u in (side, 1 - side)
        ]
        for base in range(0, groups, 2)
        for side in range(2)
    ]

    def exchange(value):
        return lax.all_to_all(
            value, AXES, split_axis=0, concat_axis=0, tiled=True, axis_index_groups=blocks
        )

    side = lax.axis_index("seq") // half_seq
    home = side == lax.axis_index("groups") % 2
    side_flag = side.astype(jnp.int32).reshape(1)
    home_flag = home.astype(jnp.int32).reshape(1)

    def shape(*dims):
        return jax.ShapeDtypeStruct(dims, jnp.bfloat16)

    heights = [own * share // 8 for share in SHARES]
    away = [(g, s, c) for g, s, c in every if not at_home(g, s)]
    low, middle, *high, first_proj, first_gain = pl.pallas_call(
        split_kernel,
        in_specs=[pl.BlockSpec(memory_space=pltpu.HBM)] * 3,
        out_specs=[pl.BlockSpec(memory_space=pltpu.VMEM)] * (len(heights) + 2),
        out_shape=[shape(height, width, channels) for height in heights]
        + [jax.ShapeDtypeStruct(value.shape, value.dtype) for value in (tri_proj, tri_gain)],
        scratch_shapes=[pltpu.SemaphoreType.DMA((len(heights) + 2,))],
        compiler_params=pltpu.CompilerParams(vmem_limit_bytes=VMEM_BYTES),
        name="split",
    )(*(
        pltpu.with_memory_space_constraint(value, pltpu.HBM)
        for value in (pair_rep, tri_proj, tri_gain)
    ))
    hopped = [permute(part, [((g, s, c), (g ^ 1, s, c)) for g, s, c in every]) for part in high]
    direct = permute(low, [((g, s, c), (g, across(s), c)) for g, s, c in away])
    relayed = [
        permute(part, [((g, s, c), (g, across(s), c)) for g, s, c in every if at_home(g, s)])
        for part in hopped
    ]
    diagonal = permute(middle, [((g, s, c), (g ^ 1, across(s), c)) for g, s, c in away])
    stepped = permute(middle, [((g, s, c), (g ^ 1, s, c)) for g, s, c in every if at_home(g, s)])

    scratch = [pltpu.VMEM((inner * rows, LANES), jnp.float32)]

    near, near_normed, near_sent = call(
        near_kernel, "project",
        [shape(own, width, channels)] * 2 + [shape(parts, 2 * per * own, width)], [],
        home_flag, low, first_gain, first_proj, stepped, *hopped, flops=0,
    )
    near_got = exchange(near_sent)
    far, far_normed, far_sent = call(
        near_kernel, "project",
        [shape(own, width, channels)] * 2 + [shape(parts, 2 * per * own, width)], [],
        home_flag, direct, first_gain, first_proj, diagonal, *relayed, flops=5 * FAR_FLOPS,
    )
    far_got = exchange(far_sent)

    product = call(
        outgoing_kernel, "outgoing", shape(parts, per, rows, width), [],
        side_flag, near_got, far_got,
    )
    back = exchange(product).reshape(parts, per * rows, width)

    current, normed, sent = call(
        middle_kernel, "combine_project",
        [shape(rows, width, channels)] * 2 + [shape(parts, 2 * per * rows, width)], scratch,
        near, far, near_normed, far_normed, back, tri_gain, tri_gate, tri_mid_gain, tri_out, tri_proj,
    )
    got = exchange(sent).reshape(parts, 2, per, rows, width)

    product = call(
        incoming_kernel, "incoming", shape(parts, per * rows, width), [], side_flag, got
    )
    back = exchange(product)

    def last(slot, back, flops):
        return call(
            functools.partial(last_kernel, slot), "combine_transition",
            shape(own, width, channels), scratch,
            current, normed, back, tri_gate, tri_mid_gain, tri_out, trans_gain[None],
            trans_up, trans_down, flops=flops,
        )

    far_out = last(1, back, 0)
    near_out = last(0, after(back, far_out), FAR_FLOPS)

    from_home = permute(
        far_out, [((g, s, c), (g, across(s), c)) for g, s, c in every if at_home(g, s)]
    )
    from_away = permute(
        far_out, [((g, s, c), (g ^ 1, across(s), c)) for g, s, c in every if not at_home(g, s)]
    )
    from_near = permute(
        near_out, [((g, s, c), (g ^ 1, s, c)) for g, s, c in every if not at_home(g, s)]
    )
    far = call(join_kernel, "join", shape(rows, width, channels), [], from_away, from_home)
    return call(
        pick_kernel, "pick", shape(rows, width, channels), [], home_flag, near_out, from_near, far
    )


def solution(mesh):
    in_specs = (P(AXES, None, None), P(), P(), P(), P(), P(), P(), P(), P())
    out_specs = P(AXES, None, None)
    return jax.shard_map(local, mesh=mesh, in_specs=in_specs, out_specs=out_specs, check_vma=False)
```
